256 devices in a mesh: seq: 64 (over x, z, core), doc: 4 (over y).
Axes of the slice: x: 4, y: 4, z: 8, core: 2. Of those that a mesh axis runs over, the one named last changes fastest.
Arguments:
- lin_query: bfloat16 [65536, 256], P(('doc', 'seq')), parts along dimension 0, may hold values from -6 to 6
- lin_key: bfloat16 [65536, 256], P(('doc', 'seq')), parts along dimension 0, may hold values from -6 to 6
- lin_value: bfloat16 [65536, 1024], P(('doc', 'seq')), parts along dimension 0, may hold values from -6 to 6
- win_query: bfloat16 [65536, 512], P(('doc', 'seq')), parts along dimension 0, may hold values from -27 to 27
- win_key: bfloat16 [65536, 512], P(('doc', 'seq')), parts along dimension 0, may hold values from -27 to 27
- win_value: bfloat16 [65536, 512], P(('doc', 'seq')), parts along dimension 0, may hold values from -6 to 6
- head_gain: float32 [1024], replicated, may hold values from 0.1 to 1.9
- out_weight: bfloat16 [1536, 1024], replicated, may hold values from -0.15625 to 0.15625
Outputs:
- mixed: bfloat16 [65536, 1024], P(('doc', 'seq')), parts along dimension 0
The draws below stay inside these ranges and needn't reach their ends.
There are 4 independent parts, one for each index of `doc`. The reference program is written for one: setup_inputs(seed, part) draws one part's arguments, and reference() takes and returns one part's arrays. A program takes and returns all parts, laid end to end along the dimension named above; an argument that names none is the same for every part. Nothing has to cross between parts.
All inputs are finite; a program needn't handle non-finite values.
Results may differ from the reference program's by a relative error of at most 0.015.
Values may be sent and summed in bfloat16 or wider, within the bound.
A program may use at most 192 MiB of HBM per device.

```python
import jax
import jax.numpy as jnp
from jax import lax

MODEL = 1024
HEADS = 16
FEAT_DIM = 16
HEAD_DIM = 64
WIN_HEADS = 8
WINDOW = 2048
LIN_BLOCK = 256
TOK_DEV = 256
TOKENS = 16384
FEATS = 273


def aligned_queries(keys, free_queries, noise, lag_key):
    key_heads = keys.reshape(TOKENS, WIN_HEADS, HEAD_DIM)
    lags = jax.random.randint(lag_key, (TOKENS, WIN_HEADS), 1, WINDOW)
    sources = jnp.arange(TOKENS, dtype=jnp.int32)[:, None] - lags
    head_index = jnp.arange(WIN_HEADS, dtype=jnp.int32)[None, :]
    picked = key_heads[jnp.maximum(sources, 0), head_index, :]
    aligned = 0.6 * picked + noise.reshape(TOKENS, WIN_HEADS, HEAD_DIM)
    queries = jnp.where((sources >= 0)[:, :, None], aligned, free_queries.reshape(TOKENS, WIN_HEADS, HEAD_DIM))
    return queries.reshape(TOKENS, WIN_HEADS * HEAD_DIM)


def window_pair(key):
    base_key = jax.random.fold_in(key, 7)
    first_key = jax.random.fold_in(base_key, 0)
    second_key = jax.random.fold_in(base_key, 1)
    third_key = jax.random.fold_in(base_key, 2)
    sixth_key = jax.random.fold_in(base_key, 5)
    width = WIN_HEADS * HEAD_DIM
    keys = jnp.clip(1.7 * jax.random.normal(first_key, (TOKENS, width), jnp.float32), -5.1, 5.1)
    free_queries = jnp.clip(1.7 * jax.random.normal(second_key, (TOKENS, width), jnp.float32), -5.1, 5.1)
    noise = jnp.clip(1.4 * jax.random.normal(third_key, (TOKENS, width), jnp.float32), -4.2, 4.2)
    queries = aligned_queries(keys, free_queries, noise, sixth_key)
    return (queries, keys)


def draw_win_query(key, part):
    return window_pair(key)[0].astype(jnp.bfloat16)


def draw_win_key(key, part):
    return window_pair(key)[1].astype(jnp.bfloat16)


def block_levels(stream_key, dims, shards, low, largest):
    def one(dim, parts):
        steps = jax.random.uniform(jax.random.fold_in(jax.random.fold_in(stream_key, 6), dim), (parts,), jnp.float32, low / len(shards), largest / len(shards))
        return jnp.repeat(jnp.exp(steps), dims[dim] // parts).reshape((-1,) + (1,) * (len(dims) - dim - 1))

    loudness = one(*shards[0])
    for cut in shards[1:]:
        loudness = loudness * one(*cut)
    return loudness


def gaussian(own_key, dims, spread, most, cuts=(), held_as=jnp.bfloat16):
    entries = jax.random.normal(own_key, dims, jnp.float32) * spread
    if len(cuts) > 0:
        entries = block_levels(own_key, dims, cuts, -0.22, 0.18) * entries
    return jnp.clip(entries, min=-most, max=most).astype(held_as)


def setup_inputs(seed: int = 0, part: int = 0) -> dict:
    streams_of = jax.random.split(jax.random.key(seed), 9)
    part_splits = jax.random.split(jax.random.fold_in(streams_of[8], part), 9)
    lin_query = gaussian(part_splits[0], (TOKENS, HEADS * FEAT_DIM), 1.0, 6.0, ((0, 64),))
    lin_key = gaussian(part_splits[1], (TOKENS, HEADS * FEAT_DIM), 1.0, 6.0, ((0, 64),))
    lin_value = gaussian(part_splits[2], (TOKENS, HEADS * HEAD_DIM), 1.0, 6.0, ((0, 64),))
    win_query = draw_win_query(jax.random.fold_in(jax.random.fold_in(streams_of[8], part), 71), part)
    win_key = draw_win_key(jax.random.fold_in(jax.random.fold_in(streams_of[8], part), 71), part)
    win_value = gaussian(part_splits[5], (TOKENS, WIN_HEADS * HEAD_DIM), 1.0, 6.0, ((0, 64),))
    head_gain = jnp.clip(1.0 + 0.18 * jax.random.normal(streams_of[6], (HEADS * HEAD_DIM,), jnp.float32), 0.1, 1.9)
    out_weight = gaussian(streams_of[7], ((HEADS + WIN_HEADS) * HEAD_DIM, MODEL), ((HEADS + WIN_HEADS) * HEAD_DIM) ** -0.5, 0.15625)
    return dict(lin_query=lin_query, lin_key=lin_key, lin_value=lin_value, win_query=win_query, win_key=win_key, win_value=win_value, head_gain=head_gain, out_weight=out_weight)


def round_trip(values):
    return lax.optimization_barrier(values.astype(jnp.bfloat16)).astype(jnp.float32)

def taylor_features(input_rows):
    row_count = input_rows.shape[0]
    pieces = input_rows.astype(jnp.float32).reshape(row_count, HEADS, FEAT_DIM)
    square = (pieces[:, :, :, None] * pieces[:, :, None, :]).reshape(row_count, HEADS, FEAT_DIM * FEAT_DIM)
    first = jnp.ones((row_count, HEADS, 1), jnp.float32)
    return jnp.concatenate([first, pieces * FEAT_DIM ** (-0.25), square * (2.0 * FEAT_DIM) ** (-0.5)], axis=2)

def linear_branch(lin_query, lin_key, lin_value, head_gain):
    block_count = TOKENS // LIN_BLOCK
    query_blocks = lin_query.reshape(block_count, LIN_BLOCK, HEADS * FEAT_DIM)
    key_blocks = lin_key.reshape(block_count, LIN_BLOCK, HEADS * FEAT_DIM)
    value_blocks = lin_value.reshape(block_count, LIN_BLOCK, HEADS * HEAD_DIM)
    causal = jnp.arange(LIN_BLOCK, dtype=jnp.int32)[:, None] >= jnp.arange(LIN_BLOCK, dtype=jnp.int32)[None, :]

    def one_block(state, pieces):
        query_rows, key_rows, value_rows = pieces
        feat_query = round_trip(taylor_features(query_rows))
        feat_key = round_trip(taylor_features(key_rows))
        values = value_rows.astype(jnp.float32).reshape(LIN_BLOCK, HEADS, HEAD_DIM)
        weights = jnp.einsum('rhf,shf->hrs', feat_query, feat_key)
        weights = round_trip(jnp.where(causal[None], weights, 0.0))
        intra = jnp.einsum('hrs,she->rhe', weights, values)
        prior = round_trip(state)
        inter = jnp.einsum('rhf,hfe->rhe', feat_query, prior)
        state = state + jnp.einsum('shf,she->hfe', feat_key, values)
        return (state, intra + inter)
    start_state = jnp.zeros((HEADS, FEATS, HEAD_DIM), jnp.float32)
    final_state, numer = lax.scan(one_block, start_state, (query_blocks, key_blocks, value_blocks))
    numer = numer.reshape(TOKENS, HEADS, HEAD_DIM)
    scaled = numer * lax.rsqrt(lax.optimization_barrier(jnp.mean(numer * numer, axis=2, keepdims=True)) + 1e-05)
    scaled = scaled * head_gain.reshape(HEADS, HEAD_DIM)
    return scaled.astype(jnp.bfloat16).reshape(TOKENS, HEADS * HEAD_DIM)

def window_branch(win_query, win_key, win_value):
    block_rows = min(512, TOK_DEV)
    key_span = WINDOW + block_rows
    width = WIN_HEADS * HEAD_DIM
    padding = jnp.zeros((WINDOW, width), jnp.bfloat16)
    keys = jnp.concatenate([padding, win_key], axis=0)
    values = jnp.concatenate([padding, win_value], axis=0)
    starts = jnp.arange(TOKENS // block_rows, dtype=jnp.int32) * block_rows
    query_pos = jnp.arange(block_rows, dtype=jnp.int32)[:, None]
    key_pos = jnp.arange(key_span, dtype=jnp.int32)[None, :]

    def one_block(block_start):
        query_rows = lax.dynamic_slice_in_dim(win_query, block_start, block_rows, 0).astype(jnp.float32).reshape(block_rows, WIN_HEADS, HEAD_DIM)
        key_rows = lax.dynamic_slice_in_dim(keys, block_start, key_span, 0).astype(jnp.float32).reshape(key_span, WIN_HEADS, HEAD_DIM)
        value_rows = lax.dynamic_slice_in_dim(values, block_start, key_span, 0).astype(jnp.float32).reshape(key_span, WIN_HEADS, HEAD_DIM)
        scores = jnp.einsum('rhd,thd->hrt', query_rows, key_rows) * HEAD_DIM ** (-0.5)
        allowed = (key_pos > query_pos) & (key_pos <= query_pos + WINDOW) & (block_start - WINDOW + key_pos >= 0)
        scores = jnp.where(allowed[None], scores, -1e+30)
        highest = lax.optimization_barrier(jnp.max(scores, axis=2, keepdims=True))
        weights = jnp.where(allowed[None], jnp.exp(scores - highest), 0.0)
        totals = lax.optimization_barrier(jnp.sum(weights, axis=2, keepdims=True))
        probs = round_trip(weights / totals)
        result = jnp.einsum('hrt,thd->rhd', probs, value_rows)
        return result.astype(jnp.bfloat16).reshape(block_rows, width)
    return lax.map(one_block, starts).reshape(TOKENS, width)

def reference(lin_query, lin_key, lin_value, win_query, win_key, win_value, head_gain, out_weight):
    linear_out = linear_branch(lin_query, lin_key, lin_value, head_gain)
    window_out = window_branch(win_query, win_key, win_value)
    joined = jnp.concatenate([linear_out, window_out], axis=1)
    return jnp.dot(joined, out_weight, preferred_element_type=jnp.float32).astype(jnp.bfloat16)
```

```python
import functools

import jax
import jax.numpy as jnp
from jax import lax
from jax.experimental import pallas as pl
from jax.experimental.pallas import tpu as pltpu
from jax.sharding import PartitionSpec as P

HEADS = 16
FEAT_DIM = 16
HEAD_DIM = 64
WIN_HEADS = 8
WINDOW = 2048
ROWS = 256
FEATS = 160
HALF = FEATS // 2
LINE = 16
CHIPS = 8
PAIR = 2 * HEAD_DIM
SLOTS = 16
SPAN = WINDOW + ROWS
MESH = pl.DeviceIdType.MESH
F32 = jnp.float32
BF16 = jnp.bfloat16


def taylor_rows(x):
    rows = [x * x * (2.0 * FEAT_DIM) ** (-0.5)]
    for shift in range(1, 8):
        rows.append(x * pltpu.roll(x, FEAT_DIM - shift, 0) * 0.25)
    last = x[0:8] * x[8:16] * 0.25
    place = lax.broadcasted_iota(jnp.int32, last.shape, 0)
    rows.append(last)
    rows.append(jnp.where(place == 0, 1.0, 0.0))
    rows.append(x * 0.5)
    return jnp.concatenate(rows, axis=0).astype(BF16)


def layer_kernel(
    lines,
    lq_ref, lk_ref, lv_ref, wq_ref, wk_ref, wv_ref, gain_ref, weight_hbm, out_ref,
    weight, qv_out, kt_out, qv, kt, vo,
    q_t, k_t, v_t, feat_q, numer, lin_out,
    s_own, s_other, s_chip, s_line, t_own, t_line, pre_out, pre_in, d2d_out, prior,
    o_out, o_in, acc,
    weight_sem, qv_ss, qv_rs, kt_ss, kt_rs, rqv_ss, rkt_ss, o_ss, o_rs,
    s0_ss, s0_rs, s1_ss, s1_rs, s2_ss, s2_rs, s3_ss, s3_rs, s4_ss, s4_rs,
):
    me = lax.axis_index("seq")
    line = me // LINE
    place = me % LINE
    chip = place // 2
    core = place % 2
    owner_core = place // 8
    base = line * LINE

    def remote(src, dst, ss, rs, target):
        return pltpu.make_async_remote_copy(
            src_ref=src, dst_ref=dst, send_sem=ss, recv_sem=rs,
            device_id={"seq": target}, device_id_type=MESH,
        )

    barrier = pltpu.get_barrier_semaphore()
    for step in range(1, LINE):
        pl.semaphore_signal(
            barrier, inc=1, device_id={"seq": base + (place + step) % LINE}, device_id_type=MESH
        )
    for step in range(1, lines):
        for other in range(2):
            target = ((line + step) % lines) * LINE + chip * 2 + other
            pl.semaphore_signal(barrier, inc=1, device_id={"seq": target}, device_id_type=MESH)

    weight_copy = pltpu.make_async_copy(weight_hbm, weight, weight_sem)
    weight_copy.start()

    lane = lax.broadcasted_iota(jnp.int32, (ROWS, PAIR), 1)
    for pair in range(4):
        cols = slice(pair * PAIR, (pair + 1) * PAIR)
        q_pair = wq_ref[:, cols].astype(F32)
        v_pair = wv_ref[:, cols].astype(F32)
        qv_out[2 * pair] = jnp.where(lane < HEAD_DIM, q_pair, pltpu.roll(v_pair, HEAD_DIM, 1)).astype(BF16)
        qv_out[2 * pair + 1] = jnp.where(lane < HEAD_DIM, pltpu.roll(q_pair, HEAD_DIM, 1), v_pair).astype(BF16)
    for head in range(WIN_HEADS // 2):
        cols = slice(head * PAIR, (head + 1) * PAIR)
        turned = wk_ref[:, cols].astype(F32).T.astype(BF16)
        kt_out[2 * head] = turned[:HEAD_DIM]
        kt_out[2 * head + 1] = turned[HEAD_DIM:]
    kt[HEAD_DIM:, :] = jnp.zeros((HEAD_DIM, SLOTS * ROWS), BF16)

    q_t[...] = lq_ref[...].astype(F32).T
    k_t[...] = lk_ref[...].astype(F32).T

    def pair_state(pair, carry):
        values = lv_ref[:, pl.ds(pl.multiple_of(pair * PAIR, PAIR), PAIR)]
        first = taylor_rows(k_t[pl.ds(pl.multiple_of(pair * 32, 32), 16), :])
        second = taylor_rows(k_t[pl.ds(pl.multiple_of(pair * 32 + 16, 16), 16), :])
        s_first = jnp.dot(first, values, preferred_element_type=F32)
        s_second = jnp.dot(second, values, preferred_element_type=F32)
        lanes = lax.broadcasted_iota(jnp.int32, (FEATS, PAIR), 1)
        state = jnp.where(lanes < HEAD_DIM, s_first, s_second).astype(BF16)
        s_own[0, pair] = state[:HALF]
        s_own[1, pair] = state[HALF:]
        return carry

    lax.fori_loop(0, CHIPS, pair_state, 0)

    pl.semaphore_wait(barrier, LINE - 1 + 2 * (lines - 1))

    s0 = remote(s_own.at[1 - core], s_other, s0_ss, s0_rs, me + 1 - 2 * core)
    s0.start()

    my_slot = 8 + place % 8
    my_cols = pl.ds(pl.multiple_of(my_slot * ROWS, ROWS), ROWS)

    def window_copies(step):
        target_chip = (chip + step) % CHIPS
        target = base + target_chip * 2 + owner_core
        return (
            remote(kt_out.at[target_chip], kt.at[0:HEAD_DIM, my_cols], kt_ss.at[step], kt_rs.at[my_slot], target),
            remote(qv_out.at[target_chip], qv.at[my_slot], qv_ss.at[step], qv_rs.at[my_slot], target),
        )

    stays = owner_core == core
    order = (1, 7, 2, 6, 3, 5, 4)

    s0.wait()
    for pair in range(CHIPS):
        s_chip[pair] = (s_own[core, pair].astype(F32) + s_other[pair].astype(F32)).astype(BF16)

    def scatter(src, dst, ss, rs, step):
        target_chip = (chip + step) % CHIPS
        return remote(src.at[target_chip], dst.at[chip], ss.at[step], rs.at[step], base + target_chip * 2 + core)

    for step in order:
        scatter(s_chip, s_line, s1_ss, s1_rs, step).start()
    s_line[chip] = s_chip[chip]

    for step in order:
        for copy in window_copies(step):
            copy.start()

    @pl.when(jnp.logical_not(stays))
    def _():
        for copy in window_copies(0):
            copy.start()

    @pl.when(stays)
    def _():
        kt[0:HEAD_DIM, my_cols] = kt_out[chip]
        qv[my_slot] = qv_out[chip]

    v_t[...] = lv_ref[...].astype(F32).T.astype(BF16)
    key_pos = lax.broadcasted_iota(jnp.int32, (ROWS, ROWS), 0)
    query_pos = lax.broadcasted_iota(jnp.int32, (ROWS, ROWS), 1)
    causal = key_pos <= query_pos

    def intra(head, carry):
        feat_q[head] = taylor_rows(q_t[pl.ds(pl.multiple_of(head * 16, 16), 16), :])
        group = head // 8
        rows = pl.ds(pl.multiple_of(group * 128, 128), 128)
        row_head = lax.broadcasted_iota(jnp.int32, (128, ROWS), 0) // FEAT_DIM + group * 8
        query = jnp.where(row_head == head, q_t[rows, :], 0.0).astype(BF16)
        dots = jnp.dot(lk_ref[:, rows], query, preferred_element_type=F32)
        pair_weight = jnp.where(causal, 1.0 + dots * (0.25 + dots * (1.0 / 32.0)), 0.0).astype(BF16)
        own = pl.ds(pl.multiple_of(head * HEAD_DIM, HEAD_DIM), HEAD_DIM)
        numer[own, :] = jnp.dot(v_t[own, :], pair_weight, preferred_element_type=F32)
        return carry

    lax.fori_loop(0, HEADS, intra, 0)

    for step in order:
        scatter(s_chip, s_line, s1_ss, s1_rs, step).wait()
    total = s_line[0].astype(F32)
    for source in range(1, CHIPS):
        total = total + s_line[source].astype(F32)
    t_own[...] = total.astype(BF16)

    def line_copy(step):
        target = ((line + step) % lines) * LINE + place
        return remote(t_own, t_line.at[step - 1], s2_ss.at[step - 1], s2_rs.at[step - 1], target)

    for step in range(1, lines):
        line_copy(step).start()
    for step in range(1, lines):
        line_copy(step).wait()
    running = jnp.zeros((HALF, PAIR), F32)
    for step in range(1, lines):
        running = running + jnp.where(line >= step, t_line[step - 1].astype(F32), 0.0)
    for target in range(CHIPS):
        pre_out[target] = running.astype(BF16)
        running = running + s_line[target].astype(F32)
    for step in order:
        scatter(pre_out, pre_in, s3_ss, s3_rs, step).start()
    pre_in[chip] = pre_out[chip]
    for step in order:
        scatter(pre_out, pre_in, s3_ss, s3_rs, step).wait()
    for pair in range(CHIPS):
        before = pre_in[pair].astype(F32)
        d2d_out[pair] = (before + jnp.where(core == 0, s_own[0, pair].astype(F32), 0.0)).astype(BF16)
        prior[core, pair] = (before + jnp.where(core == 1, s_other[pair].astype(F32), 0.0)).astype(BF16)
    s4 = remote(d2d_out, prior.at[core], s4_ss, s4_rs, me + 1 - 2 * core)
    s4.start()
    s4.wait()

    gain_t = gain_ref[...].T

    def inter(pair, carry):
        state = jnp.concatenate([prior[0, pair], prior[1, pair]], axis=0)
        state_t = state.astype(F32).T.astype(BF16)
        pair_lane = lax.broadcasted_iota(jnp.int32, gain_t.shape, 1)
        gains = jnp.sum(jnp.where(pair_lane == pair, gain_t, 0.0), axis=1, keepdims=True)
        for half in range(2):
            head = 2 * pair + half
            own = pl.ds(pl.multiple_of(head * HEAD_DIM, HEAD_DIM), HEAD_DIM)
            rows = slice(half * HEAD_DIM, (half + 1) * HEAD_DIM)
            value = numer[own, :] + jnp.dot(state_t[rows], feat_q[head], preferred_element_type=F32)
            spread = jnp.sum(value * value, axis=0, keepdims=True) * (1.0 / HEAD_DIM)
            scaled = value * lax.rsqrt(spread + 1e-05) * gains[rows]
            numer[own, :] = scaled
        cols = pl.ds(pl.multiple_of(pair * PAIR, PAIR), PAIR)
        lin_out[:, cols] = numer[cols, :].T.astype(BF16)
        return carry

    lax.fori_loop(0, CHIPS, inter, 0)
    weight_copy.wait()
    split = HEADS * HEAD_DIM
    acc[...] = jnp.dot(lin_out[...], weight[:split], preferred_element_type=F32)

    passes_on = jnp.logical_or(core == 0, line + 1 < lines)
    next_device = me + 1 + (LINE - 2) * core
    ones_lane = lax.broadcasted_iota(jnp.int32, (ROWS, PAIR), 1) < HEAD_DIM

    def slot_cols(slot):
        return pl.ds(pl.multiple_of(slot * ROWS, ROWS), ROWS)

    def arrival(slot):
        return (
            remote(kt_out.at[0], kt.at[0:HEAD_DIM, slot_cols(slot)], kt_ss.at[0], kt_rs.at[slot], me),
            remote(qv_out.at[0], qv.at[slot], qv_ss.at[0], qv_rs.at[slot], me),
        )

    def onward(index):
        return (
            remote(kt.at[0:HEAD_DIM, slot_cols(8 + index)], kt.at[0:HEAD_DIM, slot_cols(index)],
                   rkt_ss.at[index], kt_rs.at[index], next_device),
            remote(qv.at[8 + index], qv.at[index], rqv_ss.at[index], qv_rs.at[index], next_device),
        )

    def with_ones(slot):
        vo[slot_cols(slot), :] = jnp.where(ones_lane, 1.0, qv[slot].astype(F32)).astype(BF16)

    def pass_on(turn, carry):
        index = 7 - turn

        @pl.when(8 * core + index != place)
        def _():
            for copy in arrival(8 + index):
                copy.wait_recv()

        @pl.when(passes_on)
        def _():
            for copy in onward(index):
                copy.start()

        with_ones(8 + index)
        return carry

    lax.fori_loop(0, 8, pass_on, 0)

    has_earlier = jnp.logical_or(core == 1, line > 0)

    @pl.when(jnp.logical_not(has_earlier))
    def _():
        first_key = kt[0:HEAD_DIM, 8 * ROWS : 8 * ROWS + 128].astype(F32)[:, 0:1]
        kt[0:HEAD_DIM, 0 : 8 * ROWS] = jnp.broadcast_to(first_key, (HEAD_DIM, 8 * ROWS)).astype(BF16)
        vo[0 : 8 * ROWS, :] = jnp.zeros((8 * ROWS, PAIR), BF16)

    row = lax.broadcasted_iota(jnp.int32, (ROWS, ROWS), 0)
    col = lax.broadcasted_iota(jnp.int32, (ROWS, ROWS), 1)
    exp_scale = HEAD_DIM ** (-0.5) * 1.4426950408889634

    def output_copy(index):
        return remote(o_out.at[index], o_in.at[chip], o_ss.at[index], o_rs.at[chip], base + 8 * core + index)

    def attend(turn, carry):
        index = 7 - turn

        @pl.when(has_earlier)
        def _():
            for copy in arrival(index):
                copy.wait_recv()
            with_ones(index)

        span = pl.ds(pl.multiple_of(index * ROWS, ROWS), SPAN)
        scores = jnp.dot(qv[8 + index], kt[:, span], preferred_element_type=F32)
        oldest = jnp.where(col > row, scores[:, :ROWS], -1e30)
        newest = jnp.where(col <= row, scores[:, WINDOW:], -1e30)
        scores = jnp.concatenate([oldest, scores[:, ROWS:WINDOW], newest], axis=1)
        highest = jnp.max(scores, axis=1, keepdims=True)
        weights = jnp.exp2((scores - highest) * exp_scale).astype(BF16)
        sums = jnp.dot(weights, vo[span, :], preferred_element_type=F32)
        result = sums / pltpu.roll(sums, HEAD_DIM, 1)
        half_lane = lax.broadcasted_iota(jnp.int32, (128, PAIR), 1)
        packed = jnp.where(half_lane < HEAD_DIM, pltpu.roll(result[:128], HEAD_DIM, 1), result[128:])
        o_out[index] = packed.astype(BF16)

        @pl.when(8 * core + index != place)
        def _():
            output_copy(index).start()

        @pl.when(8 * core + index == place)
        def _():
            o_in[chip] = o_out[index]

        return carry

    lax.fori_loop(0, 8, attend, 0)

    for head in range(WIN_HEADS):

        @pl.when(jnp.logical_or(head != chip, jnp.logical_not(stays)))
        def _():
            remote(o_out.at[0], o_in.at[head], o_ss.at[0], o_rs.at[head], me).wait_recv()

    half_lane = lax.broadcasted_iota(jnp.int32, (128, PAIR), 1)
    tops, bottoms = [], []
    for pair in range(4):
        first = o_in[2 * pair].astype(F32)
        second = o_in[2 * pair + 1].astype(F32)
        tops.append(jnp.where(half_lane < HEAD_DIM, first, pltpu.roll(second, HEAD_DIM, 1)).astype(BF16))
        bottoms.append(jnp.where(half_lane < HEAD_DIM, pltpu.roll(first, HEAD_DIM, 1), second).astype(BF16))
    window_out = jnp.concatenate(
        [jnp.concatenate(tops, axis=1), jnp.concatenate(bottoms, axis=1)], axis=0
    )
    out_ref[...] = (acc[...] + jnp.dot(window_out, weight[split:], preferred_element_type=F32)).astype(BF16)

    for step in order:
        for copy in window_copies(step):
            copy.wait_send()

    @pl.when(jnp.logical_not(stays))
    def _():
        for copy in window_copies(0):
            copy.wait_send()

    @pl.when(passes_on)
    def _():
        for index in range(8):
            for copy in onward(index):
                copy.wait_send()

    for index in range(8):

        @pl.when(8 * core + index != place)
        def _():
            output_copy(index).wait_send()


def per_device(lin_query, lin_key, lin_value, win_query, win_key, win_value, head_gain, out_weight):
    lines = lax.axis_size("seq") // LINE
    vmem = pl.BlockSpec(memory_space=pltpu.VMEM)
    dma = pltpu.SemaphoreType.DMA
    width = HEADS * HEAD_DIM
    scratch = [
        pltpu.VMEM(out_weight.shape, BF16),
        pltpu.VMEM((WIN_HEADS, ROWS, PAIR), BF16),
        pltpu.VMEM((WIN_HEADS, HEAD_DIM, ROWS), BF16),
        pltpu.VMEM((SLOTS, ROWS, PAIR), BF16),
        pltpu.VMEM((2 * HEAD_DIM, SLOTS * ROWS), BF16),
        pltpu.VMEM((SLOTS * ROWS, PAIR), BF16),
        pltpu.VMEM((ROWS, ROWS), F32),
        pltpu.VMEM((ROWS, ROWS), F32),
        pltpu.VMEM((width, ROWS), BF16),
        pltpu.VMEM((HEADS, FEATS, ROWS), BF16),
        pltpu.VMEM((width, ROWS), F32),
        pltpu.VMEM((ROWS, width), BF16),
        pltpu.VMEM((2, CHIPS, HALF, PAIR), BF16),
        pltpu.VMEM((CHIPS, HALF, PAIR), BF16),
        pltpu.VMEM((CHIPS, HALF, PAIR), BF16),
        pltpu.VMEM((CHIPS, HALF, PAIR), BF16),
        pltpu.VMEM((HALF, PAIR), BF16),
        pltpu.VMEM((lines - 1, HALF, PAIR), BF16),
        pltpu.VMEM((CHIPS, HALF, PAIR), BF16),
        pltpu.VMEM((CHIPS, HALF, PAIR), BF16),
        pltpu.VMEM((CHIPS, HALF, PAIR), BF16),
        pltpu.VMEM((2, CHIPS, HALF, PAIR), BF16),
        pltpu.VMEM((8, 128, PAIR), BF16),
        pltpu.VMEM((WIN_HEADS, 128, PAIR), BF16),
        pltpu.VMEM((ROWS, out_weight.shape[1]), F32),
        dma(()),
        dma((8,)), dma((SLOTS,)), dma((8,)), dma((SLOTS,)), dma((8,)), dma((8,)), dma((8,)), dma((8,)),
        dma(()), dma(()),
        dma((8,)), dma((8,)),
        dma((lines - 1,)), dma((lines - 1,)),
        dma((8,)), dma((8,)),
        dma(()), dma(()),
    ]
    return pl.pallas_call(
        functools.partial(layer_kernel, lines),
        out_shape=jax.ShapeDtypeStruct((ROWS, out_weight.shape[1]), BF16),
        in_specs=[vmem] * 7 + [pl.BlockSpec(memory_space=pl.ANY)],
        out_specs=vmem,
        scratch_shapes=scratch,
        name="layer_pair",
        compiler_params=pltpu.CompilerParams(
            collective_id=0, has_side_effects=True, vmem_limit_bytes=56 * 2**20
        ),
    )(lin_query, lin_key, lin_value, win_query, win_key, win_value, head_gain.reshape(8, 128), out_weight)


def solution(mesh):
    rows = P(("doc", "seq"), None)
    return jax.shard_map(
        per_device,
        mesh=mesh,
        in_specs=(rows, rows, rows, rows, rows, rows, P(), P()),
        out_specs=rows,
        check_vma=False,
    )
```

```python
import functools

import jax
import jax.numpy as jnp
from jax import lax
from jax.experimental import pallas as pl
from jax.experimental.pallas import tpu as pltpu
from jax.sharding import PartitionSpec as P

HEADS = 16
FEAT_DIM = 16
HEAD_DIM = 64
WIN_HEADS = 8
WINDOW = 2048
ROWS = 256
FEATS = 160
HALF = FEATS // 2
LINE = 16
CHIPS = 8
PAIR = 2 * HEAD_DIM
SLOTS = 16
SPAN = WINDOW + ROWS
MESH = pl.DeviceIdType.MESH
F32 = jnp.float32
BF16 = jnp.bfloat16


def taylor_rows(x):
    rows = [x * x * (2.0 * FEAT_DIM) ** (-0.5)]
    for shift in range(1, 8):
        rows.append(x * pltpu.roll(x, FEAT_DIM - shift, 0) * 0.25)
    last = x[0:8] * x[8:16] * 0.25
    place = lax.broadcasted_iota(jnp.int32, last.shape, 0)
    rows.append(last)
    rows.append(jnp.where(place == 0, 1.0, 0.0))
    rows.append(x * 0.5)
    return jnp.concatenate(rows, axis=0).astype(BF16)


def layer_kernel(
    lines,
    lq_hbm, lk_hbm, lv_hbm, wq_hbm, wk_hbm, wv_hbm, gain_ref, weight_hbm, out_ref,
    lq_ref, lk_ref, lv_ref, wq_ref, wk_ref, wv_ref, weight, kv_out, qp_out, kv, qp, kt, vo,
    q_t, k_t, v_t, feat_q, numer, lin_out,
    s_own, s_other, s_chip, s_line, t_own, t_line, pre_out, pre_in, d2d_out, prior,
    o_out, o_in, acc, scores_a, scores_b,
    load_sem, kv_ss, kv_rs, qp_ss, qp_rs, on_ss, o_ss, o_rs,
    s0_ss, s0_rs, s1_ss, s1_rs, s2_ss, s2_rs, s3_ss, s3_rs, s4_ss, s4_rs,
):
    me = lax.axis_index("seq")
    line = me // LINE
    place = me % LINE
    chip = place // 2
    core = place % 2
    owner_core = place // 8
    base = line * LINE

    def remote(src, dst, ss, rs, target):
        return pltpu.make_async_remote_copy(
            src_ref=src, dst_ref=dst, send_sem=ss, recv_sem=rs,
            device_id={"seq": target}, device_id_type=MESH,
        )

    sources = (wk_hbm, wv_hbm, wq_hbm, lk_hbm, lv_hbm, lq_hbm, weight_hbm)
    places = (wk_ref, wv_ref, wq_ref, lk_ref, lv_ref, lq_ref, weight)
    loads = [pltpu.make_async_copy(a, b, load_sem.at[i]) for i, (a, b) in enumerate(zip(sources, places))]
    load_wk, load_wv, load_wq, load_lk, load_lv, load_lq, load_weight = loads
    for load in loads:
        load.start()

    barrier = pltpu.get_barrier_semaphore()
    for step in range(1, LINE):
        pl.semaphore_signal(
            barrier, inc=1, device_id={"seq": base + (place + step) % LINE}, device_id_type=MESH
        )
    for step in range(1, lines):
        for other in range(2):
            target = ((line + step) % lines) * LINE + chip * 2 + other
            pl.semaphore_signal(barrier, inc=1, device_id={"seq": target}, device_id_type=MESH)

    half_lane = lax.broadcasted_iota(jnp.int32, (ROWS // 2, PAIR), 1) < HEAD_DIM

    def side_by_side(pair):
        top, bottom = pair[: ROWS // 2], pair[ROWS // 2 :]
        first = jnp.where(half_lane, top, pltpu.roll(bottom, HEAD_DIM, 1))
        second = jnp.where(half_lane, pltpu.roll(top, HEAD_DIM, 1), bottom)
        return first.astype(BF16), second.astype(BF16)

    load_wk.wait()
    load_wv.wait()
    for pair in range(WIN_HEADS // 2):
        cols = slice(pair * PAIR, (pair + 1) * PAIR)
        turned = wk_ref[:, cols].astype(F32).T.astype(BF16)
        values = side_by_side(wv_ref[:, cols].astype(F32))
        for half in range(2):
            rows = slice(half * HEAD_DIM, (half + 1) * HEAD_DIM)
            kv_out[2 * pair + half, 0:64] = turned[rows, :128]
            kv_out[2 * pair + half, 64:128] = turned[rows, 128:]
            kv_out[2 * pair + half, 128:256] = values[half]

    pl.semaphore_wait(barrier, LINE - 1 + 2 * (lines - 1))

    my_slot = place % 8

    def kv_copy(step):
        target_chip = (chip + step) % CHIPS
        target = base + target_chip * 2 + owner_core
        return remote(kv_out.at[target_chip], kv.at[8 + my_slot], kv_ss.at[step], kv_rs.at[8 + my_slot], target)

    def qp_copy(step):
        target_chip = (chip + step) % CHIPS
        target = base + target_chip * 2 + owner_core
        return remote(qp_out.at[target_chip], qp.at[my_slot], qp_ss.at[step], qp_rs.at[my_slot], target)

    stays = owner_core == core
    order = (1, 7, 2, 6, 3, 5, 4)

    for step in order[: 4]:
        kv_copy(step).start()

    @pl.when(jnp.logical_not(stays))
    def _():
        kv_copy(0).start()

    @pl.when(stays)
    def _():
        kv[8 + my_slot] = kv_out[chip]

    load_lk.wait()
    load_lv.wait()
    k_t[...] = lk_ref[...].astype(F32).T

    def pair_state(pair, carry):
        values = lv_ref[:, pl.ds(pl.multiple_of(pair * PAIR, PAIR), PAIR)]
        first = taylor_rows(k_t[pl.ds(pl.multiple_of(pair * 32, 32), 16), :])
        second = taylor_rows(k_t[pl.ds(pl.multiple_of(pair * 32 + 16, 16), 16), :])
        s_first = jnp.dot(first, values, preferred_element_type=F32)
        s_second = jnp.dot(second, values, preferred_element_type=F32)
        lanes = lax.broadcasted_iota(jnp.int32, (FEATS, PAIR), 1)
        state = jnp.where(lanes < HEAD_DIM, s_first, s_second).astype(BF16)
        s_own[0, pair] = state[:HALF]
        s_own[1, pair] = state[HALF:]
        return carry

    lax.fori_loop(0, CHIPS, pair_state, 0)

    s0 = remote(s_own.at[1 - core], s_other, s0_ss, s0_rs, me + 1 - 2 * core)
    s0.start()

    load_wq.wait()
    for pair in range(WIN_HEADS // 2):
        queries = side_by_side(wq_ref[:, pair * PAIR : (pair + 1) * PAIR].astype(F32))
        qp_out[2 * pair] = queries[0]
        qp_out[2 * pair + 1] = queries[1]

    @pl.when(stays)
    def _():
        qp[my_slot] = qp_out[chip]

    def send_queries():
        for step in order:
            qp_copy(step).start()

        @pl.when(jnp.logical_not(stays))
        def _():
            qp_copy(0).start()

    s0.wait()
    for pair in range(CHIPS):
        s_chip[pair] = (s_own[core, pair].astype(F32) + s_other[pair].astype(F32)).astype(BF16)

    def scatter(src, dst, ss, rs, step):
        target_chip = (chip + step) % CHIPS
        return remote(src.at[target_chip], dst.at[chip], ss.at[step], rs.at[step], base + target_chip * 2 + core)

    for step in order:
        scatter(s_chip, s_line, s1_ss, s1_rs, step).start()
    for step in order[4 :]:
        kv_copy(step).start()
    s_line[chip] = s_chip[chip]

    send_queries()
    load_lq.wait()
    q_t[...] = lq_ref[...].astype(F32).T
    v_t[...] = lv_ref[...].astype(F32).T.astype(BF16)
    key_pos = lax.broadcasted_iota(jnp.int32, (ROWS, ROWS), 0)
    query_pos = lax.broadcasted_iota(jnp.int32, (ROWS, ROWS), 1)
    causal = key_pos <= query_pos

    def intra(head, carry):
        feat_q[head] = taylor_rows(q_t[pl.ds(pl.multiple_of(head * 16, 16), 16), :])
        group = head // 8
        rows = pl.ds(pl.multiple_of(group * 128, 128), 128)
        row_head = lax.broadcasted_iota(jnp.int32, (128, ROWS), 0) // FEAT_DIM + group * 8
        query = jnp.where(row_head == head, q_t[rows, :], 0.0).astype(BF16)
        dots = jnp.dot(lk_ref[:, rows], query, preferred_element_type=F32)
        pair_weight = jnp.where(causal, 1.0 + dots * (0.25 + dots * (1.0 / 32.0)), 0.0).astype(BF16)
        own = pl.ds(pl.multiple_of(head * HEAD_DIM, HEAD_DIM), HEAD_DIM)
        numer[own, :] = jnp.dot(v_t[own, :], pair_weight, preferred_element_type=F32)
        return carry

    lax.fori_loop(0, HEADS, intra, 0, unroll=4)
    kt[HEAD_DIM:, :] = jnp.zeros((HEAD_DIM, SLOTS * ROWS), BF16)

    passes_on = jnp.logical_or(core == 0, line + 1 < lines)
    next_device = me + 1 + (LINE - 2) * core

    def slot_cols(slot):
        return pl.ds(pl.multiple_of(slot * ROWS, ROWS), ROWS)

    def arrival(slot):
        return remote(kv_out.at[0], kv.at[slot], kv_ss.at[0], kv_rs.at[slot], me)

    def onward(index):
        return remote(kv.at[8 + index], kv.at[index], on_ss.at[index], kv_rs.at[index], next_device)

    def unpack(slot):
        start = slot * ROWS
        low = pl.ds(pl.multiple_of(start, 128), 128)
        high = pl.ds(pl.multiple_of(start + 128, 128), 128)
        kt[0:HEAD_DIM, low] = kv[slot, 0:64]
        kt[0:HEAD_DIM, high] = kv[slot, 64:128]
        values = kv[slot, 128:256].astype(F32)
        vo[low, :] = jnp.where(half_lane, 1.0, pltpu.roll(values, HEAD_DIM, 1)).astype(BF16)
        vo[high, :] = jnp.where(half_lane, 1.0, values).astype(BF16)

    offset = (chip - 4 * core + CHIPS) % CHIPS
    ranks = [sorted(range(4), key=lambda k: min((u - k) % 8, (k - u) % 8)) for u in range(CHIPS)]
    code = 0
    for u in range(CHIPS):
        code = code + jnp.where(offset == u, sum(k * 4**t for t, k in enumerate(ranks[u])), 0)

    def pass_on(turn, carry):
        digit = turn // 2
        divisor = jnp.where(digit == 0, 1, jnp.where(digit == 1, 4, jnp.where(digit == 2, 16, 64)))
        index = (code // divisor) % 4 * 2 + turn % 2

        @pl.when(8 * core + index != place)
        def _():
            arrival(8 + index).wait_recv()

        @pl.when(passes_on)
        def _():
            onward(index).start()

        unpack(8 + index)
        return carry

    lax.fori_loop(0, 8, pass_on, 0)

    has_earlier = jnp.logical_or(core == 1, line > 0)

    @pl.when(jnp.logical_not(has_earlier))
    def _():
        first_key = kt[0:HEAD_DIM, 8 * ROWS : 8 * ROWS + 128].astype(F32)[:, 0:1]
        kt[0:HEAD_DIM, 0 : 8 * ROWS] = jnp.broadcast_to(first_key, (HEAD_DIM, 8 * ROWS)).astype(BF16)
        vo[0 : 8 * ROWS, :] = jnp.zeros((8 * ROWS, PAIR), BF16)

    def inter_all():
        for step in order:
            scatter(pre_out, pre_in, s3_ss, s3_rs, step).wait()
        for pair in range(CHIPS):
            before = pre_in[pair].astype(F32)
            d2d_out[pair] = (before + jnp.where(core == 0, s_own[0, pair].astype(F32), 0.0)).astype(BF16)
            prior[core, pair] = (before + jnp.where(core == 1, s_other[pair].astype(F32), 0.0)).astype(BF16)
        s4 = remote(d2d_out, prior.at[core], s4_ss, s4_rs, me + 1 - 2 * core)
        s4.start()
        s4.wait()

        gain_t = gain_ref[...].T

        def inter(pair, carry):
            state = jnp.concatenate([prior[0, pair], prior[1, pair]], axis=0)
            state_t = state.astype(F32).T.astype(BF16)
            pair_lane = lax.broadcasted_iota(jnp.int32, gain_t.shape, 1)
            gains = jnp.sum(jnp.where(pair_lane == pair, gain_t, 0.0), axis=1, keepdims=True)
            for half in range(2):
                head = 2 * pair + half
                own = pl.ds(pl.multiple_of(head * HEAD_DIM, HEAD_DIM), HEAD_DIM)
                rows = slice(half * HEAD_DIM, (half + 1) * HEAD_DIM)
                value = numer[own, :] + jnp.dot(state_t[rows], feat_q[head], preferred_element_type=F32)
                spread = jnp.sum(value * value, axis=0, keepdims=True) * (1.0 / HEAD_DIM)
                scaled = value * lax.rsqrt(spread + 1e-05) * gains[rows]
                numer[own, :] = scaled
            cols = pl.ds(pl.multiple_of(pair * PAIR, PAIR), PAIR)
            lin_out[:, cols] = numer[cols, :].T.astype(BF16)
            return carry

        lax.fori_loop(0, CHIPS, inter, 0, unroll=8)
        load_weight.wait()
        split = HEADS * HEAD_DIM
        acc[...] = jnp.dot(lin_out[...], weight[:split], preferred_element_type=F32)


    row = lax.broadcasted_iota(jnp.int32, (ROWS, ROWS), 0)
    col = lax.broadcasted_iota(jnp.int32, (ROWS, ROWS), 1)
    exp_scale = HEAD_DIM ** (-0.5) * 1.4426950408889634

    def output_copy(index):
        return remote(o_out.at[index], o_in.at[chip], o_ss.at[index], o_rs.at[chip], base + 8 * core + index)

    def line_copy(step):
        target = ((line + step) % lines) * LINE + place
        return remote(t_own, t_line.at[step - 1], s2_ss.at[step - 1], s2_rs.at[step - 1], target)

    def line_totals():
        for step in order:
            scatter(s_chip, s_line, s1_ss, s1_rs, step).wait()
        total = s_line[0].astype(F32)
        for source in range(1, CHIPS):
            total = total + s_line[source].astype(F32)
        t_own[...] = total.astype(BF16)

        for step in range(1, lines):
            line_copy(step).start()

    def send_prefixes():
        for step in range(1, lines):
            line_copy(step).wait()
        running = jnp.zeros((HALF, PAIR), F32)
        for step in range(1, lines):
            running = running + jnp.where(line >= step, t_line[step - 1].astype(F32), 0.0)
        for target in range(CHIPS):
            pre_out[target] = running.astype(BF16)
            running = running + s_line[target].astype(F32)
        for step in order:
            scatter(pre_out, pre_in, s3_ss, s3_rs, step).start()
        pre_in[chip] = pre_out[chip]

    def arrive(index):
        @pl.when(has_earlier)
        def _():
            arrival(index).wait_recv()
            unpack(index)

        @pl.when(8 * core + index != place)
        def _():
            remote(qp_out.at[0], qp.at[index], qp_ss.at[0], qp_rs.at[index], me).wait_recv()

    def score(index, scores):
        packed_query = qp[index].astype(F32)
        query = jnp.concatenate([packed_query, pltpu.roll(packed_query, HEAD_DIM, 1)], axis=0).astype(BF16)
        raw = jnp.dot(query, kt[:, index * ROWS : index * ROWS + SPAN], preferred_element_type=F32)
        scores[:, :ROWS] = jnp.where(col > row, raw[:, :ROWS], -1e30)
        scores[:, ROWS:WINDOW] = raw[:, ROWS:WINDOW]
        scores[:, WINDOW:] = jnp.where(col <= row, raw[:, WINDOW:], -1e30)

    def attend(index, scores):
        highest = jnp.max(scores[...], axis=1, keepdims=True)
        weights = jnp.exp2((scores[...] - highest) * exp_scale).astype(BF16)
        sums = jnp.dot(weights, vo[index * ROWS : index * ROWS + SPAN, :], preferred_element_type=F32)
        result = sums / pltpu.roll(sums, HEAD_DIM, 1)
        packed = jnp.where(half_lane, pltpu.roll(result[:128], HEAD_DIM, 1), result[128:])
        o_out[index] = packed.astype(BF16)

    def send_output(index):
        @pl.when(8 * core + index != place)
        def _():
            output_copy(index).start()

        @pl.when(8 * core + index == place)
        def _():
            o_in[chip] = o_out[index]

    buffers = (scores_a, scores_b)
    arrive(7)
    score(7, buffers[0])
    for turn in range(8):
        index = 7 - turn
        if turn == 0:
            line_totals()
        if turn == 1:
            send_prefixes()
        if index > 0:
            arrive(index - 1)
            score(index - 1, buffers[(turn + 1) % 2])
        attend(index, buffers[turn % 2])
        send_output(index)
    inter_all()

    for head in range(WIN_HEADS):

        @pl.when(jnp.logical_or(head != chip, jnp.logical_not(stays)))
        def _():
            remote(o_out.at[0], o_in.at[head], o_ss.at[0], o_rs.at[head], me).wait_recv()

    tops, bottoms = [], []
    for pair in range(4):
        first = o_in[2 * pair].astype(F32)
        second = o_in[2 * pair + 1].astype(F32)
        tops.append(jnp.where(half_lane, first, pltpu.roll(second, HEAD_DIM, 1)).astype(BF16))
        bottoms.append(jnp.where(half_lane, pltpu.roll(first, HEAD_DIM, 1), second).astype(BF16))
    window_out = jnp.concatenate(
        [jnp.concatenate(tops, axis=1), jnp.concatenate(bottoms, axis=1)], axis=0
    )
    out_ref[...] = (acc[...] + jnp.dot(window_out, weight[HEADS * HEAD_DIM:], preferred_element_type=F32)).astype(BF16)

    for step in order:
        kv_copy(step).wait_send()
        qp_copy(step).wait_send()

    @pl.when(jnp.logical_not(stays))
    def _():
        kv_copy(0).wait_send()
        qp_copy(0).wait_send()

    @pl.when(passes_on)
    def _():
        for index in range(8):
            onward(index).wait_send()

    for index in range(8):

        @pl.when(8 * core + index != place)
        def _():
            output_copy(index).wait_send()


def per_device(lin_query, lin_key, lin_value, win_query, win_key, win_value, head_gain, out_weight):
    lines = lax.axis_size("seq") // LINE
    vmem = pl.BlockSpec(memory_space=pltpu.VMEM)
    hbm = pl.BlockSpec(memory_space=pl.ANY)
    tokens = (lin_query, lin_key, lin_value, win_query, win_key, win_value)
    dma = pltpu.SemaphoreType.DMA
    width = HEADS * HEAD_DIM
    scratch = [
        *[pltpu.VMEM(array.shape, BF16) for array in tokens],
        pltpu.VMEM(out_weight.shape, BF16),
        pltpu.VMEM((WIN_HEADS, ROWS, PAIR), BF16),
        pltpu.VMEM((WIN_HEADS, ROWS // 2, PAIR), BF16),
        pltpu.VMEM((SLOTS, ROWS, PAIR), BF16),
        pltpu.VMEM((8, ROWS // 2, PAIR), BF16),
        pltpu.VMEM((2 * HEAD_DIM, SLOTS * ROWS), BF16),
        pltpu.VMEM((SLOTS * ROWS, PAIR), BF16),
        pltpu.VMEM((ROWS, ROWS), F32),
        pltpu.VMEM((ROWS, ROWS), F32),
        pltpu.VMEM((width, ROWS), BF16),
        pltpu.VMEM((HEADS, FEATS, ROWS), BF16),
        pltpu.VMEM((width, ROWS), F32),
        pltpu.VMEM((ROWS, width), BF16),
        pltpu.VMEM((2, CHIPS, HALF, PAIR), BF16),
        pltpu.VMEM((CHIPS, HALF, PAIR), BF16),
        pltpu.VMEM((CHIPS, HALF, PAIR), BF16),
        pltpu.VMEM((CHIPS, HALF, PAIR), BF16),
        pltpu.VMEM((HALF, PAIR), BF16),
        pltpu.VMEM((lines - 1, HALF, PAIR), BF16),
        pltpu.VMEM((CHIPS, HALF, PAIR), BF16),
        pltpu.VMEM((CHIPS, HALF, PAIR), BF16),
        pltpu.VMEM((CHIPS, HALF, PAIR), BF16),
        pltpu.VMEM((2, CHIPS, HALF, PAIR), BF16),
        pltpu.VMEM((8, 128, PAIR), BF16),
        pltpu.VMEM((WIN_HEADS, 128, PAIR), BF16),
        pltpu.VMEM((ROWS, out_weight.shape[1]), F32),
        pltpu.VMEM((ROWS, SPAN), F32),
        pltpu.VMEM((ROWS, SPAN), F32),
        dma((7,)),
        dma((8,)), dma((SLOTS,)), dma((8,)), dma((8,)), dma((8,)), dma((8,)), dma((8,)),
        dma(()), dma(()),
        dma((8,)), dma((8,)),
        dma((lines - 1,)), dma((lines - 1,)),
        dma((8,)), dma((8,)),
        dma(()), dma(()),
    ]
    return pl.pallas_call(
        functools.partial(layer_kernel, lines),
        out_shape=jax.ShapeDtypeStruct((ROWS, out_weight.shape[1]), BF16),
        in_specs=[hbm] * 6 + [vmem, hbm],
        out_specs=vmem,
        scratch_shapes=scratch,
        name="layer_pair",
        compiler_params=pltpu.CompilerParams(
            collective_id=0, has_side_effects=True, vmem_limit_bytes=56 * 2**20
        ),
    )(lin_query, lin_key, lin_value, win_query, win_key, win_value, head_gain.reshape(8, 128), out_weight)


def solution(mesh):
    rows = P(("doc", "seq"), None)
    return jax.shard_map(
        per_device,
        mesh=mesh,
        in_specs=(rows, rows, rows, rows, rows, rows, P(), P()),
        out_specs=rows,
        check_vma=False,
    )
```

```python
import functools

import jax
import jax.numpy as jnp
from jax import lax
from jax.experimental import pallas as pl
from jax.experimental.pallas import tpu as pltpu
from jax.sharding import PartitionSpec as P

HEADS = 16
FEAT_DIM = 16
HEAD_DIM = 64
WIN_HEADS = 8
WINDOW = 2048
ROWS = 256
FEATS = 160
HALF = FEATS // 2
LINE = 16
CHIPS = 8
PAIR = 2 * HEAD_DIM
SLOTS = 16
SPAN = WINDOW + ROWS
MESH = pl.DeviceIdType.MESH
F32 = jnp.float32
BF16 = jnp.bfloat16


def taylor_rows(x):
    rows = [x * x * (2.0 * FEAT_DIM) ** (-0.5)]
    for shift in range(1, 8):
        rows.append(x * pltpu.roll(x, FEAT_DIM - shift, 0) * 0.25)
    last = x[0:8] * x[8:16] * 0.25
    place = lax.broadcasted_iota(jnp.int32, last.shape, 0)
    rows.append(last)
    rows.append(jnp.where(place == 0, 1.0, 0.0))
    rows.append(x * 0.5)
    return jnp.concatenate(rows, axis=0).astype(BF16)


def layer_kernel(
    lines,
    lq_hbm, lk_hbm, lv_hbm, wq_hbm, wk_hbm, wv_hbm, gain_ref, weight_hbm, out_ref,
    lq_ref, lk_ref, lv_ref, wq_ref, wk_ref, wv_ref, weight, kv_out, qp_out, kv, qp, kt, vo,
    q_t, k_t, v_t, feat_q, numer, lin_out,
    s_own, s_other, s_chip, s_line, t_own, t_line, pre_out, pre_in, d2d_out, prior,
    o_out, o_in, acc, scores_a, scores_b,
    load_sem, kv_ss, kv_rs, qp_ss, qp_rs, on_ss, o_ss, o_rs,
    s0_ss, s0_rs, s1_ss, s1_rs, s2_ss, s2_rs, s3_ss, s3_rs, s4_ss, s4_rs,
):
    me = lax.axis_index("seq")
    line = me // LINE
    place = me % LINE
    chip = place // 2
    core = place % 2
    owner_core = place // 8
    base = line * LINE

    def remote(src, dst, ss, rs, target):
        return pltpu.make_async_remote_copy(
            src_ref=src, dst_ref=dst, send_sem=ss, recv_sem=rs,
            device_id={"seq": target}, device_id_type=MESH,
        )

    sources = (wk_hbm, wv_hbm, wq_hbm, lk_hbm, lv_hbm, lq_hbm, weight_hbm)
    places = (wk_ref, wv_ref, wq_ref, lk_ref, lv_ref, lq_ref, weight)
    loads = [pltpu.make_async_copy(a, b, load_sem.at[i]) for i, (a, b) in enumerate(zip(sources, places))]
    load_wk, load_wv, load_wq, load_lk, load_lv, load_lq, load_weight = loads
    for load in loads:
        load.start()

    barrier = pltpu.get_barrier_semaphore()
    for step in range(1, LINE):
        pl.semaphore_signal(
            barrier, inc=1, device_id={"seq": base + (place + step) % LINE}, device_id_type=MESH
        )
    for step in range(1, lines):
        for other in range(2):
            target = ((line + step) % lines) * LINE + chip * 2 + other
            pl.semaphore_signal(barrier, inc=1, device_id={"seq": target}, device_id_type=MESH)

    half_lane = lax.broadcasted_iota(jnp.int32, (ROWS // 2, PAIR), 1) < HEAD_DIM

    def side_by_side(pair):
        top, bottom = pair[: ROWS // 2], pair[ROWS // 2 :]
        first = jnp.where(half_lane, top, pltpu.roll(bottom, HEAD_DIM, 1))
        second = jnp.where(half_lane, pltpu.roll(top, HEAD_DIM, 1), bottom)
        return first.astype(BF16), second.astype(BF16)

    load_wk.wait()
    load_wv.wait()
    for pair in range(WIN_HEADS // 2):
        cols = slice(pair * PAIR, (pair + 1) * PAIR)
        turned = wk_ref[:, cols].astype(F32).T.astype(BF16)
        values = side_by_side(wv_ref[:, cols].astype(F32))
        for half in range(2):
            rows = slice(half * HEAD_DIM, (half + 1) * HEAD_DIM)
            kv_out[2 * pair + half, 0:64] = turned[rows, :128]
            kv_out[2 * pair + half, 64:128] = turned[rows, 128:]
            kv_out[2 * pair + half, 128:256] = values[half]

    pl.semaphore_wait(barrier, LINE - 1 + 2 * (lines - 1))

    my_slot = place % 8

    def kv_copy(step):
        target_chip = (chip + step) % CHIPS
        target = base + target_chip * 2 + owner_core
        return remote(kv_out.at[target_chip], kv.at[8 + my_slot], kv_ss.at[step], kv_rs.at[8 + my_slot], target)

    def qp_copy(step):
        target_chip = (chip + step) % CHIPS
        target = base + target_chip * 2 + owner_core
        return remote(qp_out.at[target_chip], qp.at[my_slot], qp_ss.at[step], qp_rs.at[my_slot], target)

    stays = owner_core == core
    order = (1, 7, 2, 6, 3, 5, 4)

    for step in order[: 4]:
        kv_copy(step).start()

    @pl.when(jnp.logical_not(stays))
    def _():
        kv_copy(0).start()

    @pl.when(stays)
    def _():
        kv[8 + my_slot] = kv_out[chip]

    load_lk.wait()
    load_lv.wait()
    k_t[...] = lk_ref[...].astype(F32).T

    def pair_state(pair, carry):
        values = lv_ref[:, pl.ds(pl.multiple_of(pair * PAIR, PAIR), PAIR)]
        first = taylor_rows(k_t[pl.ds(pl.multiple_of(pair * 32, 32), 16), :])
        second = taylor_rows(k_t[pl.ds(pl.multiple_of(pair * 32 + 16, 16), 16), :])
        s_first = jnp.dot(first, values, preferred_element_type=F32)
        s_second = jnp.dot(second, values, preferred_element_type=F32)
        lanes = lax.broadcasted_iota(jnp.int32, (FEATS, PAIR), 1)
        state = jnp.where(lanes < HEAD_DIM, s_first, s_second).astype(BF16)
        s_own[0, pair] = state[:HALF]
        s_own[1, pair] = state[HALF:]
        return carry

    lax.fori_loop(0, CHIPS, pair_state, 0)

    s0 = remote(s_own.at[1 - core], s_other, s0_ss, s0_rs, me + 1 - 2 * core)
    s0.start()

    load_wq.wait()
    for pair in range(WIN_HEADS // 2):
        queries = side_by_side(wq_ref[:, pair * PAIR : (pair + 1) * PAIR].astype(F32))
        qp_out[2 * pair] = queries[0]
        qp_out[2 * pair + 1] = queries[1]

    @pl.when(stays)
    def _():
        qp[my_slot] = qp_out[chip]

    def send_queries():
        for step in order:
            qp_copy(step).start()

        @pl.when(jnp.logical_not(stays))
        def _():
            qp_copy(0).start()

    s0.wait()
    for pair in range(CHIPS):
        s_chip[pair] = (s_own[core, pair].astype(F32) + s_other[pair].astype(F32)).astype(BF16)

    def scatter(src, dst, ss, rs, step):
        target_chip = (chip + step) % CHIPS
        return remote(src.at[target_chip], dst.at[chip], ss.at[step], rs.at[step], base + target_chip * 2 + core)

    for step in order:
        scatter(s_chip, s_line, s1_ss, s1_rs, step).start()
    for step in order[4 :]:
        kv_copy(step).start()
    s_line[chip] = s_chip[chip]

    send_queries()
    load_lq.wait()
    q_t[...] = lq_ref[...].astype(F32).T
    v_t[...] = lv_ref[...].astype(F32).T.astype(BF16)
    key_pos = lax.broadcasted_iota(jnp.int32, (ROWS, ROWS), 0)
    query_pos = lax.broadcasted_iota(jnp.int32, (ROWS, ROWS), 1)
    causal = key_pos <= query_pos

    def intra(head, carry):
        feat_q[head] = taylor_rows(q_t[pl.ds(pl.multiple_of(head * 16, 16), 16), :])
        group = head // 8
        rows = pl.ds(pl.multiple_of(group * 128, 128), 128)
        row_head = lax.broadcasted_iota(jnp.int32, (128, ROWS), 0) // FEAT_DIM + group * 8
        query = jnp.where(row_head == head, q_t[rows, :], 0.0).astype(BF16)
        dots = jnp.dot(lk_ref[:, rows], query, preferred_element_type=F32)
        pair_weight = jnp.where(causal, 1.0 + dots * (0.25 + dots * (1.0 / 32.0)), 0.0).astype(BF16)
        own = pl.ds(pl.multiple_of(head * HEAD_DIM, HEAD_DIM), HEAD_DIM)
        numer[own, :] = jnp.dot(v_t[own, :], pair_weight, preferred_element_type=F32)
        return carry

    def line_copy(step):
        target = ((line + step) % lines) * LINE + place
        return remote(t_own, t_line.at[step - 1], s2_ss.at[step - 1], s2_rs.at[step - 1], target)

    def line_totals():
        for step in order:
            scatter(s_chip, s_line, s1_ss, s1_rs, step).wait()
        total = s_line[0].astype(F32)
        for source in range(1, CHIPS):
            total = total + s_line[source].astype(F32)
        t_own[...] = total.astype(BF16)

        for step in range(1, lines):
            line_copy(step).start()

    def send_prefixes():
        for step in range(1, lines):
            line_copy(step).wait()
        running = jnp.zeros((HALF, PAIR), F32)
        for step in range(1, lines):
            running = running + jnp.where(line >= step, t_line[step - 1].astype(F32), 0.0)
        for target in range(CHIPS):
            pre_out[target] = running.astype(BF16)
            running = running + s_line[target].astype(F32)
        for step in order:
            scatter(pre_out, pre_in, s3_ss, s3_rs, step).start()
        pre_in[chip] = pre_out[chip]

    lax.fori_loop(0, HEADS, intra, 0, unroll=4)
    line_totals()
    kt[HEAD_DIM:, :] = jnp.zeros((HEAD_DIM, SLOTS * ROWS), BF16)

    passes_on = jnp.logical_or(core == 0, line + 1 < lines)
    next_device = me + 1 + (LINE - 2) * core

    def slot_cols(slot):
        return pl.ds(pl.multiple_of(slot * ROWS, ROWS), ROWS)

    def arrival(slot):
        return remote(kv_out.at[0], kv.at[slot], kv_ss.at[0], kv_rs.at[slot], me)

    def onward(index):
        return remote(kv.at[8 + index], kv.at[index], on_ss.at[index], kv_rs.at[index], next_device)

    def unpack(slot):
        start = slot * ROWS
        low = pl.ds(pl.multiple_of(start, 128), 128)
        high = pl.ds(pl.multiple_of(start + 128, 128), 128)
        kt[0:HEAD_DIM, low] = kv[slot, 0:64]
        kt[0:HEAD_DIM, high] = kv[slot, 64:128]
        values = kv[slot, 128:256].astype(F32)
        vo[low, :] = jnp.where(half_lane, 1.0, pltpu.roll(values, HEAD_DIM, 1)).astype(BF16)
        vo[high, :] = jnp.where(half_lane, 1.0, values).astype(BF16)

    offset = (chip - 4 * core + CHIPS) % CHIPS
    ranks = [sorted(range(4), key=lambda k: min((u - k) % 8, (k - u) % 8)) for u in range(CHIPS)]
    code = 0
    for u in range(CHIPS):
        code = code + jnp.where(offset == u, sum(k * 4**t for t, k in enumerate(ranks[u])), 0)

    def pass_on(turn, carry):
        digit = turn // 2
        divisor = jnp.where(digit == 0, 1, jnp.where(digit == 1, 4, jnp.where(digit == 2, 16, 64)))
        index = (code // divisor) % 4 * 2 + turn % 2

        @pl.when(8 * core + index != place)
        def _():
            arrival(8 + index).wait_recv()

        @pl.when(passes_on)
        def _():
            onward(index).start()

        unpack(8 + index)
        return carry

    lax.fori_loop(0, 4, pass_on, 0)
    send_prefixes()
    lax.fori_loop(4, 8, pass_on, 0)

    has_earlier = jnp.logical_or(core == 1, line > 0)

    @pl.when(jnp.logical_not(has_earlier))
    def _():
        first_key = kt[0:HEAD_DIM, 8 * ROWS : 8 * ROWS + 128].astype(F32)[:, 0:1]
        kt[0:HEAD_DIM, 0 : 8 * ROWS] = jnp.broadcast_to(first_key, (HEAD_DIM, 8 * ROWS)).astype(BF16)
        vo[0 : 8 * ROWS, :] = jnp.zeros((8 * ROWS, PAIR), BF16)

    def inter_all():
        for step in order:
            scatter(pre_out, pre_in, s3_ss, s3_rs, step).wait()
        for pair in range(CHIPS):
            before = pre_in[pair].astype(F32)
            d2d_out[pair] = (before + jnp.where(core == 0, s_own[0, pair].astype(F32), 0.0)).astype(BF16)
            prior[core, pair] = (before + jnp.where(core == 1, s_other[pair].astype(F32), 0.0)).astype(BF16)
        s4 = remote(d2d_out, prior.at[core], s4_ss, s4_rs, me + 1 - 2 * core)
        s4.start()
        s4.wait()

        gain_t = gain_ref[...].T

        def inter(pair, carry):
            state = jnp.concatenate([prior[0, pair], prior[1, pair]], axis=0)
            state_t = state.astype(F32).T.astype(BF16)
            pair_lane = lax.broadcasted_iota(jnp.int32, gain_t.shape, 1)
            gains = jnp.sum(jnp.where(pair_lane == pair, gain_t, 0.0), axis=1, keepdims=True)
            for half in range(2):
                head = 2 * pair + half
                own = pl.ds(pl.multiple_of(head * HEAD_DIM, HEAD_DIM), HEAD_DIM)
                rows = slice(half * HEAD_DIM, (half + 1) * HEAD_DIM)
                value = numer[own, :] + jnp.dot(state_t[rows], feat_q[head], preferred_element_type=F32)
                spread = jnp.sum(value * value, axis=0, keepdims=True) * (1.0 / HEAD_DIM)
                scaled = value * lax.rsqrt(spread + 1e-05) * gains[rows]
                numer[own, :] = scaled
            cols = pl.ds(pl.multiple_of(pair * PAIR, PAIR), PAIR)
            lin_out[:, cols] = numer[cols, :].T.astype(BF16)
            return carry

        lax.fori_loop(0, CHIPS, inter, 0, unroll=8)
        load_weight.wait()
        split = HEADS * HEAD_DIM
        acc[...] = jnp.dot(lin_out[...], weight[:split], preferred_element_type=F32)


    row = lax.broadcasted_iota(jnp.int32, (ROWS, ROWS), 0)
    col = lax.broadcasted_iota(jnp.int32, (ROWS, ROWS), 1)
    exp_scale = HEAD_DIM ** (-0.5) * 1.4426950408889634

    def output_copy(index):
        return remote(o_out.at[index], o_in.at[chip], o_ss.at[index], o_rs.at[chip], base + 8 * core + index)

    def arrive(index):
        @pl.when(has_earlier)
        def _():
            arrival(index).wait_recv()
            unpack(index)

        @pl.when(8 * core + index != place)
        def _():
            remote(qp_out.at[0], qp.at[index], qp_ss.at[0], qp_rs.at[index], me).wait_recv()

    def score(index, scores):
        packed_query = qp[index].astype(F32)
        query = jnp.concatenate([packed_query, pltpu.roll(packed_query, HEAD_DIM, 1)], axis=0).astype(BF16)
        raw = jnp.dot(query, kt[:, index * ROWS : index * ROWS + SPAN], preferred_element_type=F32)
        scores[:, :ROWS] = jnp.where(col > row, raw[:, :ROWS], -1e30)
        scores[:, ROWS:WINDOW] = raw[:, ROWS:WINDOW]
        scores[:, WINDOW:] = jnp.where(col <= row, raw[:, WINDOW:], -1e30)

    def attend(index, scores):
        highest = jnp.max(scores[...], axis=1, keepdims=True)
        weights = jnp.exp2((scores[...] - highest) * exp_scale).astype(BF16)
        sums = jnp.dot(weights, vo[index * ROWS : index * ROWS + SPAN, :], preferred_element_type=F32)
        result = sums / pltpu.roll(sums, HEAD_DIM, 1)
        packed = jnp.where(half_lane, pltpu.roll(result[:128], HEAD_DIM, 1), result[128:])
        o_out[index] = packed.astype(BF16)

    def send_output(index):
        @pl.when(8 * core + index != place)
        def _():
            output_copy(index).start()

        @pl.when(8 * core + index == place)
        def _():
            o_in[chip] = o_out[index]

    buffers = (scores_a, scores_b)
    arrive(7)
    score(7, buffers[0])
    for turn in range(8):
        index = 7 - turn
        if turn == 8:
            inter_all()
        if index > 0:
            arrive(index - 1)
            score(index - 1, buffers[(turn + 1) % 2])
        attend(index, buffers[turn % 2])
        send_output(index)
    inter_all()

    for head in range(WIN_HEADS):

        @pl.when(jnp.logical_or(head != chip, jnp.logical_not(stays)))
        def _():
            remote(o_out.at[0], o_in.at[head], o_ss.at[0], o_rs.at[head], me).wait_recv()

    tops, bottoms = [], []
    for pair in range(4):
        first = o_in[2 * pair].astype(F32)
        second = o_in[2 * pair + 1].astype(F32)
        tops.append(jnp.where(half_lane, first, pltpu.roll(second, HEAD_DIM, 1)).astype(BF16))
        bottoms.append(jnp.where(half_lane, pltpu.roll(first, HEAD_DIM, 1), second).astype(BF16))
    window_out = jnp.concatenate(
        [jnp.concatenate(tops, axis=1), jnp.concatenate(bottoms, axis=1)], axis=0
    )
    out_ref[...] = (acc[...] + jnp.dot(window_out, weight[HEADS * HEAD_DIM:], preferred_element_type=F32)).astype(BF16)

    for step in order:
        kv_copy(step).wait_send()
        qp_copy(step).wait_send()

    @pl.when(jnp.logical_not(stays))
    def _():
        kv_copy(0).wait_send()
        qp_copy(0).wait_send()

    @pl.when(passes_on)
    def _():
        for index in range(8):
            onward(index).wait_send()

    for index in range(8):

        @pl.when(8 * core + index != place)
        def _():
            output_copy(index).wait_send()


def per_device(lin_query, lin_key, lin_value, win_query, win_key, win_value, head_gain, out_weight):
    lines = lax.axis_size("seq") // LINE
    vmem = pl.BlockSpec(memory_space=pltpu.VMEM)
    hbm = pl.BlockSpec(memory_space=pl.ANY)
    tokens = (lin_query, lin_key, lin_value, win_query, win_key, win_value)
    dma = pltpu.SemaphoreType.DMA
    width = HEADS * HEAD_DIM
    scratch = [
        *[pltpu.VMEM(array.shape, BF16) for array in tokens],
        pltpu.VMEM(out_weight.shape, BF16),
        pltpu.VMEM((WIN_HEADS, ROWS, PAIR), BF16),
        pltpu.VMEM((WIN_HEADS, ROWS // 2, PAIR), BF16),
        pltpu.VMEM((SLOTS, ROWS, PAIR), BF16),
        pltpu.VMEM((8, ROWS // 2, PAIR), BF16),
        pltpu.VMEM((2 * HEAD_DIM, SLOTS * ROWS), BF16),
        pltpu.VMEM((SLOTS * ROWS, PAIR), BF16),
        pltpu.VMEM((ROWS, ROWS), F32),
        pltpu.VMEM((ROWS, ROWS), F32),
        pltpu.VMEM((width, ROWS), BF16),
        pltpu.VMEM((HEADS, FEATS, ROWS), BF16),
        pltpu.VMEM((width, ROWS), F32),
        pltpu.VMEM((ROWS, width), BF16),
        pltpu.VMEM((2, CHIPS, HALF, PAIR), BF16),
        pltpu.VMEM((CHIPS, HALF, PAIR), BF16),
        pltpu.VMEM((CHIPS, HALF, PAIR), BF16),
        pltpu.VMEM((CHIPS, HALF, PAIR), BF16),
        pltpu.VMEM((HALF, PAIR), BF16),
        pltpu.VMEM((lines - 1, HALF, PAIR), BF16),
        pltpu.VMEM((CHIPS, HALF, PAIR), BF16),
        pltpu.VMEM((CHIPS, HALF, PAIR), BF16),
        pltpu.VMEM((CHIPS, HALF, PAIR), BF16),
        pltpu.VMEM((2, CHIPS, HALF, PAIR), BF16),
        pltpu.VMEM((8, 128, PAIR), BF16),
        pltpu.VMEM((WIN_HEADS, 128, PAIR), BF16),
        pltpu.VMEM((ROWS, out_weight.shape[1]), F32),
        pltpu.VMEM((ROWS, SPAN), F32),
        pltpu.VMEM((ROWS, SPAN), F32),
        dma((7,)),
        dma((8,)), dma((SLOTS,)), dma((8,)), dma((8,)), dma((8,)), dma((8,)), dma((8,)),
        dma(()), dma(()),
        dma((8,)), dma((8,)),
        dma((lines - 1,)), dma((lines - 1,)),
        dma((8,)), dma((8,)),
        dma(()), dma(()),
    ]
    return pl.pallas_call(
        functools.partial(layer_kernel, lines),
        out_shape=jax.ShapeDtypeStruct((ROWS, out_weight.shape[1]), BF16),
        in_specs=[hbm] * 6 + [vmem, hbm],
        out_specs=vmem,
        scratch_shapes=scratch,
        name="layer_pair",
        compiler_params=pltpu.CompilerParams(
            collective_id=0, has_side_effects=True, vmem_limit_bytes=56 * 2**20
        ),
    )(lin_query, lin_key, lin_value, win_query, win_key, win_value, head_gain.reshape(8, 128), out_weight)


def solution(mesh):
    rows = P(("doc", "seq"), None)
    return jax.shard_map(
        per_device,
        mesh=mesh,
        in_specs=(rows, rows, rows, rows, rows, rows, P(), P()),
        out_specs=rows,
        check_vma=False,
    )
```

```python
import functools

import jax
import jax.numpy as jnp
from jax import lax
from jax.experimental import pallas as pl
from jax.experimental.pallas import tpu as pltpu
from jax.sharding import PartitionSpec as P

HEADS = 16
FEAT_DIM = 16
HEAD_DIM = 64
WIN_HEADS = 8
WINDOW = 2048
ROWS = 256
FEATS = 160
HALF = FEATS // 2
LINE = 16
CHIPS = 8
PAIR = 2 * HEAD_DIM
SLOTS = 16
SPAN = WINDOW + ROWS
MESH = pl.DeviceIdType.MESH
F32 = jnp.float32
BF16 = jnp.bfloat16


def taylor_rows(x):
    rows = [x * x * (2.0 * FEAT_DIM) ** (-0.5)]
    for shift in range(1, 8):
        rows.append(x * pltpu.roll(x, FEAT_DIM - shift, 0) * 0.25)
    last = x[0:8] * x[8:16] * 0.25
    place = lax.broadcasted_iota(jnp.int32, last.shape, 0)
    rows.append(last)
    rows.append(jnp.where(place == 0, 1.0, 0.0))
    rows.append(x * 0.5)
    return jnp.concatenate(rows, axis=0).astype(BF16)


def layer_kernel(
    lines,
    lq_hbm, lk_hbm, lv_hbm, wq_hbm, wk_hbm, wv_hbm, gain_ref, weight_hbm, out_ref,
    lq_ref, lk_ref, lv_ref, wq_ref, wk_ref, wv_ref, weight, kv_out, qp_out, kv, qp, kt, vo,
    q_t, k_t, v_t, feat_q, numer, lin_out,
    s_own, s_other, s_chip, s_line, t_own, t_line, pre_out, pre_in, d2d_out, prior,
    o_out, o_in, acc, scores_a, scores_b,
    load_sem, kv_ss, kv_rs, qp_ss, qp_rs, on_ss, o_ss, o_rs,
    s0_ss, s0_rs, s1_ss, s1_rs, s2_ss, s2_rs, s3_ss, s3_rs, s4_ss, s4_rs,
):
    me = lax.axis_index("seq")
    line = me // LINE
    place = me % LINE
    chip = place // 2
    core = place % 2
    owner_core = place // 8
    base = line * LINE

    def remote(src, dst, ss, rs, target):
        return pltpu.make_async_remote_copy(
            src_ref=src, dst_ref=dst, send_sem=ss, recv_sem=rs,
            device_id={"seq": target}, device_id_type=MESH,
        )

    sources = (wk_hbm, wv_hbm, wq_hbm, lk_hbm, lv_hbm, lq_hbm, weight_hbm)
    places = (wk_ref, wv_ref, wq_ref, lk_ref, lv_ref, lq_ref, weight)
    loads = [pltpu.make_async_copy(a, b, load_sem.at[i]) for i, (a, b) in enumerate(zip(sources, places))]
    load_wk, load_wv, load_wq, load_lk, load_lv, load_lq, load_weight = loads
    for load in loads:
        load.start()

    barrier = pltpu.get_barrier_semaphore()
    for step in range(1, LINE):
        pl.semaphore_signal(
            barrier, inc=1, device_id={"seq": base + (place + step) % LINE}, device_id_type=MESH
        )
    for step in range(1, lines):
        for other in range(2):
            target = ((line + step) % lines) * LINE + chip * 2 + other
            pl.semaphore_signal(barrier, inc=1, device_id={"seq": target}, device_id_type=MESH)

    half_lane = lax.broadcasted_iota(jnp.int32, (ROWS // 2, PAIR), 1) < HEAD_DIM

    def side_by_side(pair):
        top, bottom = pair[: ROWS // 2], pair[ROWS // 2 :]
        first = jnp.where(half_lane, top, pltpu.roll(bottom, HEAD_DIM, 1))
        second = jnp.where(half_lane, pltpu.roll(top, HEAD_DIM, 1), bottom)
        return first.astype(BF16), second.astype(BF16)

    load_wk.wait()
    load_wv.wait()
    for pair in range(WIN_HEADS // 2):
        cols = slice(pair * PAIR, (pair + 1) * PAIR)
        turned = wk_ref[:, cols].astype(F32).T.astype(BF16)
        values = side_by_side(wv_ref[:, cols].astype(F32))
        for half in range(2):
            rows = slice(half * HEAD_DIM, (half + 1) * HEAD_DIM)
            kv_out[2 * pair + half, 0:64] = turned[rows, :128]
            kv_out[2 * pair + half, 64:128] = turned[rows, 128:]
            kv_out[2 * pair + half, 128:256] = values[half]

    pl.semaphore_wait(barrier, LINE - 1 + 2 * (lines - 1))

    my_slot = place % 8

    def kv_copy(step):
        target_chip = (chip + step) % CHIPS
        target = base + target_chip * 2 + owner_core
        return remote(kv_out.at[target_chip], kv.at[8 + my_slot], kv_ss.at[step], kv_rs.at[8 + my_slot], target)

    def qp_copy(step):
        target_chip = (chip + step) % CHIPS
        target = base + target_chip * 2 + owner_core
        return remote(qp_out.at[target_chip], qp.at[my_slot], qp_ss.at[step], qp_rs.at[my_slot], target)

    stays = owner_core == core
    order = (1, 7, 2, 6, 3, 5, 4)

    for step in order[: 4]:
        kv_copy(step).start()

    @pl.when(jnp.logical_not(stays))
    def _():
        kv_copy(0).start()

    @pl.when(stays)
    def _():
        kv[8 + my_slot] = kv_out[chip]

    load_lk.wait()
    load_lv.wait()
    k_t[...] = lk_ref[...].astype(F32).T

    def pair_state(pair, carry):
        values = lv_ref[:, pl.ds(pl.multiple_of(pair * PAIR, PAIR), PAIR)]
        first = taylor_rows(k_t[pl.ds(pl.multiple_of(pair * 32, 32), 16), :])
        second = taylor_rows(k_t[pl.ds(pl.multiple_of(pair * 32 + 16, 16), 16), :])
        s_first = jnp.dot(first, values, preferred_element_type=F32)
        s_second = jnp.dot(second, values, preferred_element_type=F32)
        lanes = lax.broadcasted_iota(jnp.int32, (FEATS, PAIR), 1)
        state = jnp.where(lanes < HEAD_DIM, s_first, s_second).astype(BF16)
        s_own[0, pair] = state[:HALF]
        s_own[1, pair] = state[HALF:]
        return carry

    lax.fori_loop(0, CHIPS, pair_state, 0, unroll=4)

    s0 = remote(s_own.at[1 - core], s_other, s0_ss, s0_rs, me + 1 - 2 * core)
    s0.start()

    load_wq.wait()
    for pair in range(WIN_HEADS // 2):
        queries = side_by_side(wq_ref[:, pair * PAIR : (pair + 1) * PAIR].astype(F32))
        qp_out[2 * pair] = queries[0]
        qp_out[2 * pair + 1] = queries[1]

    @pl.when(stays)
    def _():
        qp[my_slot] = qp_out[chip]

    def send_queries():
        for step in order:
            qp_copy(step).start()

        @pl.when(jnp.logical_not(stays))
        def _():
            qp_copy(0).start()

    s0.wait()
    for pair in range(CHIPS):
        s_chip[pair] = (s_own[core, pair].astype(F32) + s_other[pair].astype(F32)).astype(BF16)

    def scatter(src, dst, ss, rs, step):
        target_chip = (chip + step) % CHIPS
        return remote(src.at[target_chip], dst.at[chip], ss.at[step], rs.at[step], base + target_chip * 2 + core)

    for step in order:
        scatter(s_chip, s_line, s1_ss, s1_rs, step).start()
    for step in order[4 :]:
        kv_copy(step).start()
    s_line[chip] = s_chip[chip]

    send_queries()
    load_lq.wait()
    q_t[...] = lq_ref[...].astype(F32).T
    v_t[...] = lv_ref[...].astype(F32).T.astype(BF16)
    key_pos = lax.broadcasted_iota(jnp.int32, (ROWS, ROWS), 0)
    query_pos = lax.broadcasted_iota(jnp.int32, (ROWS, ROWS), 1)
    causal = key_pos <= query_pos

    def intra(head, carry):
        feat_q[head] = taylor_rows(q_t[pl.ds(pl.multiple_of(head * 16, 16), 16), :])
        group = head // 8
        rows = pl.ds(pl.multiple_of(group * 128, 128), 128)
        row_head = lax.broadcasted_iota(jnp.int32, (128, ROWS), 0) // FEAT_DIM + group * 8
        query = jnp.where(row_head == head, q_t[rows, :], 0.0).astype(BF16)
        dots = jnp.dot(lk_ref[:, rows], query, preferred_element_type=F32)
        pair_weight = jnp.where(causal, 1.0 + dots * (0.25 + dots * (1.0 / 32.0)), 0.0).astype(BF16)
        own = pl.ds(pl.multiple_of(head * HEAD_DIM, HEAD_DIM), HEAD_DIM)
        numer[own, :] = jnp.dot(v_t[own, :], pair_weight, preferred_element_type=F32)
        return carry

    def line_copy(step):
        target = ((line + step) % lines) * LINE + place
        return remote(t_own, t_line.at[step - 1], s2_ss.at[step - 1], s2_rs.at[step - 1], target)

    def line_totals():
        for step in order:
            scatter(s_chip, s_line, s1_ss, s1_rs, step).wait()
        total = s_line[0].astype(F32)
        for source in range(1, CHIPS):
            total = total + s_line[source].astype(F32)
        t_own[...] = total.astype(BF16)

        for step in range(1, lines):
            line_copy(step).start()

    def send_prefixes():
        for step in range(1, lines):
            line_copy(step).wait()
        running = jnp.zeros((HALF, PAIR), F32)
        for step in range(1, lines):
            running = running + jnp.where(line >= step, t_line[step - 1].astype(F32), 0.0)
        for target in range(CHIPS):
            pre_out[target] = running.astype(BF16)
            running = running + s_line[target].astype(F32)
        for step in order:
            scatter(pre_out, pre_in, s3_ss, s3_rs, step).start()
        pre_in[chip] = pre_out[chip]

    lax.fori_loop(0, HEADS, intra, 0, unroll=4)
    line_totals()
    kt[HEAD_DIM:, :] = jnp.zeros((HEAD_DIM, SLOTS * ROWS), BF16)

    passes_on = jnp.logical_or(core == 0, line + 1 < lines)
    next_device = me + 1 + (LINE - 2) * core

    def slot_cols(slot):
        return pl.ds(pl.multiple_of(slot * ROWS, ROWS), ROWS)

    def arrival(slot):
        return remote(kv_out.at[0], kv.at[slot], kv_ss.at[0], kv_rs.at[slot], me)

    def onward(index):
        return remote(kv.at[8 + index], kv.at[index], on_ss.at[index], kv_rs.at[index], next_device)

    def unpack(slot):
        start = slot * ROWS
        low = pl.ds(pl.multiple_of(start, 128), 128)
        high = pl.ds(pl.multiple_of(start + 128, 128), 128)
        kt[0:HEAD_DIM, low] = kv[slot, 0:64]
        kt[0:HEAD_DIM, high] = kv[slot, 64:128]
        values = kv[slot, 128:256].astype(F32)
        vo[low, :] = jnp.where(half_lane, 1.0, pltpu.roll(values, HEAD_DIM, 1)).astype(BF16)
        vo[high, :] = jnp.where(half_lane, 1.0, values).astype(BF16)

    offset = (chip - 4 * core + CHIPS) % CHIPS
    ranks = [sorted(range(4), key=lambda k: min((u - k) % 8, (k - u) % 8)) for u in range(CHIPS)]
    code = 0
    for u in range(CHIPS):
        code = code + jnp.where(offset == u, sum(k * 4**t for t, k in enumerate(ranks[u])), 0)

    def pass_on(turn, carry):
        digit = turn // 2
        divisor = jnp.where(digit == 0, 1, jnp.where(digit == 1, 4, jnp.where(digit == 2, 16, 64)))
        index = (code // divisor) % 4 * 2 + turn % 2

        @pl.when(8 * core + index != place)
        def _():
            arrival(8 + index).wait_recv()

        @pl.when(passes_on)
        def _():
            onward(index).start()

        unpack(8 + index)
        return carry

    lax.fori_loop(0, 4, pass_on, 0)
    send_prefixes()
    lax.fori_loop(4, 8, pass_on, 0)

    has_earlier = jnp.logical_or(core == 1, line > 0)

    @pl.when(jnp.logical_not(has_earlier))
    def _():
        first_key = kt[0:HEAD_DIM, 8 * ROWS : 8 * ROWS + 128].astype(F32)[:, 0:1]
        kt[0:HEAD_DIM, 0 : 8 * ROWS] = jnp.broadcast_to(first_key, (HEAD_DIM, 8 * ROWS)).astype(BF16)
        vo[0 : 8 * ROWS, :] = jnp.zeros((8 * ROWS, PAIR), BF16)

    def inter_all():
        for step in order:
            scatter(pre_out, pre_in, s3_ss, s3_rs, step).wait()
        for pair in range(CHIPS):
            before = pre_in[pair].astype(F32)
            d2d_out[pair] = (before + jnp.where(core == 0, s_own[0, pair].astype(F32), 0.0)).astype(BF16)
            prior[core, pair] = (before + jnp.where(core == 1, s_other[pair].astype(F32), 0.0)).astype(BF16)
        s4 = remote(d2d_out, prior.at[core], s4_ss, s4_rs, me + 1 - 2 * core)
        s4.start()
        s4.wait()

        gain_t = gain_ref[...].T

        def inter(pair, carry):
            state = jnp.concatenate([prior[0, pair], prior[1, pair]], axis=0)
            state_t = state.astype(F32).T.astype(BF16)
            pair_lane = lax.broadcasted_iota(jnp.int32, gain_t.shape, 1)
            gains = jnp.sum(jnp.where(pair_lane == pair, gain_t, 0.0), axis=1, keepdims=True)
            for half in range(2):
                head = 2 * pair + half
                own = pl.ds(pl.multiple_of(head * HEAD_DIM, HEAD_DIM), HEAD_DIM)
                rows = slice(half * HEAD_DIM, (half + 1) * HEAD_DIM)
                value = numer[own, :] + jnp.dot(state_t[rows], feat_q[head], preferred_element_type=F32)
                spread = jnp.sum(value * value, axis=0, keepdims=True) * (1.0 / HEAD_DIM)
                scaled = value * lax.rsqrt(spread + 1e-05) * gains[rows]
                numer[own, :] = scaled
            cols = pl.ds(pl.multiple_of(pair * PAIR, PAIR), PAIR)
            lin_out[:, cols] = numer[cols, :].T.astype(BF16)
            return carry

        lax.fori_loop(0, CHIPS, inter, 0, unroll=8)
        load_weight.wait()
        split = HEADS * HEAD_DIM
        acc[...] = jnp.dot(lin_out[...], weight[:split], preferred_element_type=F32)


    row = lax.broadcasted_iota(jnp.int32, (ROWS, ROWS), 0)
    col = lax.broadcasted_iota(jnp.int32, (ROWS, ROWS), 1)
    exp_scale = HEAD_DIM ** (-0.5) * 1.4426950408889634

    def output_copy(index):
        return remote(o_out.at[index], o_in.at[chip], o_ss.at[index], o_rs.at[chip], base + 8 * core + index)

    def arrive(index):
        @pl.when(has_earlier)
        def _():
            arrival(index).wait_recv()
            unpack(index)

        @pl.when(8 * core + index != place)
        def _():
            remote(qp_out.at[0], qp.at[index], qp_ss.at[0], qp_rs.at[index], me).wait_recv()

    def score(index, scores):
        packed_query = qp[index].astype(F32)
        query = jnp.concatenate([packed_query, pltpu.roll(packed_query, HEAD_DIM, 1)], axis=0).astype(BF16)
        raw = jnp.dot(query, kt[:, index * ROWS : index * ROWS + SPAN], preferred_element_type=F32)
        scores[:, :ROWS] = jnp.where(col > row, raw[:, :ROWS], -1e30)
        scores[:, ROWS:WINDOW] = raw[:, ROWS:WINDOW]
        scores[:, WINDOW:] = jnp.where(col <= row, raw[:, WINDOW:], -1e30)

    def attend(index, scores):
        highest = jnp.max(scores[...], axis=1, keepdims=True)
        weights = jnp.exp2((scores[...] - highest) * exp_scale).astype(BF16)
        sums = jnp.dot(weights, vo[index * ROWS : index * ROWS + SPAN, :], preferred_element_type=F32)
        result = sums / pltpu.roll(sums, HEAD_DIM, 1)
        packed = jnp.where(half_lane, pltpu.roll(result[:128], HEAD_DIM, 1), result[128:])
        o_out[index] = packed.astype(BF16)

    def send_output(index):
        @pl.when(8 * core + index != place)
        def _():
            output_copy(index).start()

        @pl.when(8 * core + index == place)
        def _():
            o_in[chip] = o_out[index]

    buffers = (scores_a, scores_b)
    arrive(7)
    score(7, buffers[0])
    for turn in range(8):
        index = 7 - turn
        if turn == 8:
            inter_all()
        if index > 0:
            arrive(index - 1)
            score(index - 1, buffers[(turn + 1) % 2])
        attend(index, buffers[turn % 2])
        send_output(index)
    inter_all()

    for head in range(WIN_HEADS):

        @pl.when(jnp.logical_or(head != chip, jnp.logical_not(stays)))
        def _():
            remote(o_out.at[0], o_in.at[head], o_ss.at[0], o_rs.at[head], me).wait_recv()

    tops, bottoms = [], []
    for pair in range(4):
        first = o_in[2 * pair].astype(F32)
        second = o_in[2 * pair + 1].astype(F32)
        tops.append(jnp.where(half_lane, first, pltpu.roll(second, HEAD_DIM, 1)).astype(BF16))
        bottoms.append(jnp.where(half_lane, pltpu.roll(first, HEAD_DIM, 1), second).astype(BF16))
    window_out = jnp.concatenate(
        [jnp.concatenate(tops, axis=1), jnp.concatenate(bottoms, axis=1)], axis=0
    )
    out_ref[...] = (acc[...] + jnp.dot(window_out, weight[HEADS * HEAD_DIM:], preferred_element_type=F32)).astype(BF16)

    for step in order:
        kv_copy(step).wait_send()
        qp_copy(step).wait_send()

    @pl.when(jnp.logical_not(stays))
    def _():
        kv_copy(0).wait_send()
        qp_copy(0).wait_send()

    @pl.when(passes_on)
    def _():
        for index in range(8):
            onward(index).wait_send()

    for index in range(8):

        @pl.when(8 * core + index != place)
        def _():
            output_copy(index).wait_send()


def per_device(lin_query, lin_key, lin_value, win_query, win_key, win_value, head_gain, out_weight):
    lines = lax.axis_size("seq") // LINE
    vmem = pl.BlockSpec(memory_space=pltpu.VMEM)
    hbm = pl.BlockSpec(memory_space=pl.ANY)
    tokens = (lin_query, lin_key, lin_value, win_query, win_key, win_value)
    dma = pltpu.SemaphoreType.DMA
    width = HEADS * HEAD_DIM
    scratch = [
        *[pltpu.VMEM(array.shape, BF16) for array in tokens],
        pltpu.VMEM(out_weight.shape, BF16),
        pltpu.VMEM((WIN_HEADS, ROWS, PAIR), BF16),
        pltpu.VMEM((WIN_HEADS, ROWS // 2, PAIR), BF16),
        pltpu.VMEM((SLOTS, ROWS, PAIR), BF16),
        pltpu.VMEM((8, ROWS // 2, PAIR), BF16),
        pltpu.VMEM((2 * HEAD_DIM, SLOTS * ROWS), BF16),
        pltpu.VMEM((SLOTS * ROWS, PAIR), BF16),
        pltpu.VMEM((ROWS, ROWS), F32),
        pltpu.VMEM((ROWS, ROWS), F32),
        pltpu.VMEM((width, ROWS), BF16),
        pltpu.VMEM((HEADS, FEATS, ROWS), BF16),
        pltpu.VMEM((width, ROWS), F32),
        pltpu.VMEM((ROWS, width), BF16),
        pltpu.VMEM((2, CHIPS, HALF, PAIR), BF16),
        pltpu.VMEM((CHIPS, HALF, PAIR), BF16),
        pltpu.VMEM((CHIPS, HALF, PAIR), BF16),
        pltpu.VMEM((CHIPS, HALF, PAIR), BF16),
        pltpu.VMEM((HALF, PAIR), BF16),
        pltpu.VMEM((lines - 1, HALF, PAIR), BF16),
        pltpu.VMEM((CHIPS, HALF, PAIR), BF16),
        pltpu.VMEM((CHIPS, HALF, PAIR), BF16),
        pltpu.VMEM((CHIPS, HALF, PAIR), BF16),
        pltpu.VMEM((2, CHIPS, HALF, PAIR), BF16),
        pltpu.VMEM((8, 128, PAIR), BF16),
        pltpu.VMEM((WIN_HEADS, 128, PAIR), BF16),
        pltpu.VMEM((ROWS, out_weight.shape[1]), F32),
        pltpu.VMEM((ROWS, SPAN), F32),
        pltpu.VMEM((ROWS, SPAN), F32),
        dma((7,)),
        dma((8,)), dma((SLOTS,)), dma((8,)), dma((8,)), dma((8,)), dma((8,)), dma((8,)),
        dma(()), dma(()),
        dma((8,)), dma((8,)),
        dma((lines - 1,)), dma((lines - 1,)),
        dma((8,)), dma((8,)),
        dma(()), dma(()),
    ]
    return pl.pallas_call(
        functools.partial(layer_kernel, lines),
        out_shape=pltpu.VMEM((ROWS, out_weight.shape[1]), BF16),
        in_specs=[hbm] * 6 + [vmem, hbm],
        out_specs=vmem,
        scratch_shapes=scratch,
        name="layer_pair",
        compiler_params=pltpu.CompilerParams(
            collective_id=0, has_side_effects=True, vmem_limit_bytes=56 * 2**20
        ),
    )(lin_query, lin_key, lin_value, win_query, win_key, win_value, head_gain.reshape(8, 128), out_weight)


def solution(mesh):
    rows = P(("doc", "seq"), None)
    return jax.shard_map(
        per_device,
        mesh=mesh,
        in_specs=(rows, rows, rows, rows, rows, rows, P(), P()),
        out_specs=rows,
        check_vma=False,
    )
```

```python
import functools

import jax
import jax.numpy as jnp
from jax import lax
from jax.experimental import pallas as pl
from jax.experimental.pallas import tpu as pltpu
from jax.sharding import PartitionSpec as P

HEADS = 16
FEAT_DIM = 16
HEAD_DIM = 64
WIN_HEADS = 8
WINDOW = 2048
ROWS = 256
FEATS = 160
HALF = FEATS // 2
LINE = 16
CHIPS = 8
PAIR = 2 * HEAD_DIM
SLOTS = 16
SPAN = WINDOW + ROWS
MESH = pl.DeviceIdType.MESH
F32 = jnp.float32
BF16 = jnp.bfloat16


def taylor_rows(x):
    rows = [x * x * (2.0 * FEAT_DIM) ** (-0.5)]
    for shift in range(1, 8):
        rows.append(x * pltpu.roll(x, FEAT_DIM - shift, 0) * 0.25)
    last = x[0:8] * x[8:16] * 0.25
    place = lax.broadcasted_iota(jnp.int32, last.shape, 0)
    rows.append(last)
    rows.append(jnp.where(place == 0, 1.0, 0.0))
    rows.append(x * 0.5)
    return jnp.concatenate(rows, axis=0).astype(BF16)


def layer_kernel(
    lines,
    lq_hbm, lk_hbm, lv_hbm, wq_hbm, wk_hbm, wv_hbm, gain_ref, weight_hbm, out_ref,
    lq_ref, lk_ref, lv_ref, wq_ref, wk_ref, wv_ref, weight, kv_out, qp_out, kv, qp, kt, vo,
    q_t, k_t, v_t, feat_q, numer, lin_out,
    s_own, s_other, s_chip, s_line, t_own, t_line, pre_out, pre_in, d2d_out, prior,
    o_out, o_in, acc, scores_a, scores_b,
    load_sem, kv_ss, kv_rs, qp_ss, qp_rs, on_ss, o_ss, o_rs,
    s0_ss, s0_rs, s1_ss, s1_rs, s2_ss, s2_rs, s3_ss, s3_rs, s4_ss, s4_rs,
):
    me = lax.axis_index("seq")
    line = me // LINE
    place = me % LINE
    chip = place // 2
    core = place % 2
    owner_core = place // 8
    base = line * LINE

    def remote(src, dst, ss, rs, target):
        return pltpu.make_async_remote_copy(
            src_ref=src, dst_ref=dst, send_sem=ss, recv_sem=rs,
            device_id={"seq": target}, device_id_type=MESH,
        )

    sources = (wk_hbm, wv_hbm, wq_hbm, lk_hbm, lv_hbm, lq_hbm, weight_hbm)
    places = (wk_ref, wv_ref, wq_ref, lk_ref, lv_ref, lq_ref, weight)
    loads = [pltpu.make_async_copy(a, b, load_sem.at[i]) for i, (a, b) in enumerate(zip(sources, places))]
    load_wk, load_wv, load_wq, load_lk, load_lv, load_lq, load_weight = loads
    for load in loads:
        load.start()

    barrier = pltpu.get_barrier_semaphore()
    for step in range(1, LINE):
        pl.semaphore_signal(
            barrier, inc=1, device_id={"seq": base + (place + step) % LINE}, device_id_type=MESH
        )
    for step in range(1, lines):
        for other in range(2):
            target = ((line + step) % lines) * LINE + chip * 2 + other
            pl.semaphore_signal(barrier, inc=1, device_id={"seq": target}, device_id_type=MESH)

    half_lane = lax.broadcasted_iota(jnp.int32, (ROWS // 2, PAIR), 1) < HEAD_DIM

    def side_by_side(pair):
        top, bottom = pair[: ROWS // 2], pair[ROWS // 2 :]
        first = jnp.where(half_lane, top, pltpu.roll(bottom, HEAD_DIM, 1))
        second = jnp.where(half_lane, pltpu.roll(top, HEAD_DIM, 1), bottom)
        return first.astype(BF16), second.astype(BF16)

    load_wk.wait()
    load_wv.wait()
    for pair in range(WIN_HEADS // 2):
        cols = slice(pair * PAIR, (pair + 1) * PAIR)
        turned = wk_ref[:, cols].astype(F32).T.astype(BF16)
        values = side_by_side(wv_ref[:, cols].astype(F32))
        for half in range(2):
            rows = slice(half * HEAD_DIM, (half + 1) * HEAD_DIM)
            kv_out[2 * pair + half, 0:64] = turned[rows, :128]
            kv_out[2 * pair + half, 64:128] = turned[rows, 128:]
            kv_out[2 * pair + half, 128:256] = values[half]

    pl.semaphore_wait(barrier, LINE - 1 + 2 * (lines - 1))

    my_slot = place % 8

    def kv_copy(step):
        target_chip = (chip + step) % CHIPS
        target = base + target_chip * 2 + owner_core
        return remote(kv_out.at[target_chip], kv.at[8 + my_slot], kv_ss.at[step], kv_rs.at[8 + my_slot], target)

    def qp_copy(step):
        target_chip = (chip + step) % CHIPS
        target = base + target_chip * 2 + owner_core
        return remote(qp_out.at[target_chip], qp.at[my_slot], qp_ss.at[step], qp_rs.at[my_slot], target)

    stays = owner_core == core
    order = (1, 7, 2, 6, 3, 5, 4)

    for step in order[: 4]:
        kv_copy(step).start()

    @pl.when(jnp.logical_not(stays))
    def _():
        kv_copy(0).start()

    @pl.when(stays)
    def _():
        kv[8 + my_slot] = kv_out[chip]

    load_lk.wait()
    load_lv.wait()
    k_t[...] = lk_ref[...].astype(F32).T

    def pair_state(pair, carry):
        values = lv_ref[:, pl.ds(pl.multiple_of(pair * PAIR, PAIR), PAIR)]
        first = taylor_rows(k_t[pl.ds(pl.multiple_of(pair * 32, 32), 16), :])
        second = taylor_rows(k_t[pl.ds(pl.multiple_of(pair * 32 + 16, 16), 16), :])
        s_first = jnp.dot(first, values, preferred_element_type=F32)
        s_second = jnp.dot(second, values, preferred_element_type=F32)
        lanes = lax.broadcasted_iota(jnp.int32, (FEATS, PAIR), 1)
        state = jnp.where(lanes < HEAD_DIM, s_first, s_second).astype(BF16)
        s_own[0, pair] = state[:HALF]
        s_own[1, pair] = state[HALF:]
        return carry

    lax.fori_loop(0, CHIPS, pair_state, 0, unroll=4)

    s0 = remote(s_own.at[1 - core], s_other, s0_ss, s0_rs, me + 1 - 2 * core)
    s0.start()

    load_wq.wait()
    for pair in range(WIN_HEADS // 2):
        queries = side_by_side(wq_ref[:, pair * PAIR : (pair + 1) * PAIR].astype(F32))
        qp_out[2 * pair] = queries[0]
        qp_out[2 * pair + 1] = queries[1]

    @pl.when(stays)
    def _():
        qp[my_slot] = qp_out[chip]

    def send_queries():
        for step in order:
            qp_copy(step).start()

        @pl.when(jnp.logical_not(stays))
        def _():
            qp_copy(0).start()

    s0.wait()
    for pair in range(CHIPS):
        s_chip[pair] = (s_own[core, pair].astype(F32) + s_other[pair].astype(F32)).astype(BF16)

    def scatter(src, dst, ss, rs, step):
        target_chip = (chip + step) % CHIPS
        return remote(src.at[target_chip], dst.at[chip], ss.at[step], rs.at[step], base + target_chip * 2 + core)

    for step in order:
        scatter(s_chip, s_line, s1_ss, s1_rs, step).start()
    for step in order[4 :]:
        kv_copy(step).start()
    s_line[chip] = s_chip[chip]

    send_queries()
    load_lq.wait()
    q_t[...] = lq_ref[...].astype(F32).T
    v_t[...] = lv_ref[...].astype(F32).T.astype(BF16)
    key_pos = lax.broadcasted_iota(jnp.int32, (ROWS, ROWS), 0)
    query_pos = lax.broadcasted_iota(jnp.int32, (ROWS, ROWS), 1)
    causal = key_pos <= query_pos

    def intra(head, carry):
        feat_q[head] = taylor_rows(q_t[pl.ds(pl.multiple_of(head * 16, 16), 16), :])
        group = head // 8
        rows = pl.ds(pl.multiple_of(group * 128, 128), 128)
        row_head = lax.broadcasted_iota(jnp.int32, (128, ROWS), 0) // FEAT_DIM + group * 8
        query = jnp.where(row_head == head, q_t[rows, :], 0.0).astype(BF16)
        dots = jnp.dot(lk_ref[:, rows], query, preferred_element_type=F32)
        pair_weight = jnp.where(causal, 1.0 + dots * (0.25 + dots * (1.0 / 32.0)), 0.0).astype(BF16)
        own = pl.ds(pl.multiple_of(head * HEAD_DIM, HEAD_DIM), HEAD_DIM)
        numer[own, :] = jnp.dot(v_t[own, :], pair_weight, preferred_element_type=F32)
        return carry

    def line_copy(step):
        target = ((line + step) % lines) * LINE + place
        return remote(t_own, t_line.at[step - 1], s2_ss.at[step - 1], s2_rs.at[step - 1], target)

    def line_totals():
        for step in order:
            scatter(s_chip, s_line, s1_ss, s1_rs, step).wait()
        total = s_line[0].astype(F32)
        for source in range(1, CHIPS):
            total = total + s_line[source].astype(F32)
        t_own[...] = total.astype(BF16)

        for step in range(1, lines):
            line_copy(step).start()

    def send_prefixes():
        for step in range(1, lines):
            line_copy(step).wait()
        running = jnp.zeros((HALF, PAIR), F32)
        for step in range(1, lines):
            running = running + jnp.where(line >= step, t_line[step - 1].astype(F32), 0.0)
        for target in range(CHIPS):
            pre_out[target] = running.astype(BF16)
            running = running + s_line[target].astype(F32)
        for step in order:
            scatter(pre_out, pre_in, s3_ss, s3_rs, step).start()
        pre_in[chip] = pre_out[chip]

    lax.fori_loop(0, HEADS, intra, 0, unroll=4)
    line_totals()
    kt[HEAD_DIM:, :] = jnp.zeros((HEAD_DIM, SLOTS * ROWS), BF16)

    passes_on = jnp.logical_or(core == 0, line + 1 < lines)
    next_device = me + 1 + (LINE - 2) * core

    def slot_cols(slot):
        return pl.ds(pl.multiple_of(slot * ROWS, ROWS), ROWS)

    def arrival(slot):
        return remote(kv_out.at[0], kv.at[slot], kv_ss.at[0], kv_rs.at[slot], me)

    def onward(index):
        return remote(kv.at[8 + index], kv.at[index], on_ss.at[index], kv_rs.at[index], next_device)

    def unpack(slot):
        start = slot * ROWS
        low = pl.ds(pl.multiple_of(start, 128), 128)
        high = pl.ds(pl.multiple_of(start + 128, 128), 128)
        kt[0:HEAD_DIM, low] = kv[slot, 0:64]
        kt[0:HEAD_DIM, high] = kv[slot, 64:128]
        values = kv[slot, 128:256].astype(F32)
        vo[low, :] = jnp.where(half_lane, 1.0, pltpu.roll(values, HEAD_DIM, 1)).astype(BF16)
        vo[high, :] = jnp.where(half_lane, 1.0, values).astype(BF16)

    offset = (chip - 4 * core + CHIPS) % CHIPS
    ranks = [sorted(range(4), key=lambda k: min((u - k) % 8, (k - u) % 8)) for u in range(CHIPS)]
    code = 0
    for u in range(CHIPS):
        code = code + jnp.where(offset == u, sum(k * 4**t for t, k in enumerate(ranks[u])), 0)

    def pass_on(turn, carry):
        digit = turn // 2
        divisor = jnp.where(digit == 0, 1, jnp.where(digit == 1, 4, jnp.where(digit == 2, 16, 64)))
        index = (code // divisor) % 4 * 2 + turn % 2

        @pl.when(8 * core + index != place)
        def _():
            arrival(8 + index).wait_recv()

        @pl.when(passes_on)
        def _():
            onward(index).start()

        unpack(8 + index)
        return carry

    lax.fori_loop(0, 4, pass_on, 0)
    send_prefixes()
    lax.fori_loop(4, 8, pass_on, 0)

    has_earlier = jnp.logical_or(core == 1, line > 0)

    @pl.when(jnp.logical_not(has_earlier))
    def _():
        first_key = kt[0:HEAD_DIM, 8 * ROWS : 8 * ROWS + 128].astype(F32)[:, 0:1]
        kt[0:HEAD_DIM, 0 : 8 * ROWS] = jnp.broadcast_to(first_key, (HEAD_DIM, 8 * ROWS)).astype(BF16)
        vo[0 : 8 * ROWS, :] = jnp.zeros((8 * ROWS, PAIR), BF16)

    def inter_all():
        for step in order:
            scatter(pre_out, pre_in, s3_ss, s3_rs, step).wait()
        for pair in range(CHIPS):
            before = pre_in[pair].astype(F32)
            d2d_out[pair] = (before + jnp.where(core == 0, s_own[0, pair].astype(F32), 0.0)).astype(BF16)
            prior[core, pair] = (before + jnp.where(core == 1, s_other[pair].astype(F32), 0.0)).astype(BF16)
        s4 = remote(d2d_out, prior.at[core], s4_ss, s4_rs, me + 1 - 2 * core)
        s4.start()
        s4.wait()

        gain_t = gain_ref[...].T

        def inter(pair, carry):
            state = jnp.concatenate([prior[0, pair], prior[1, pair]], axis=0)
            state_t = state.astype(F32).T.astype(BF16)
            pair_lane = lax.broadcasted_iota(jnp.int32, gain_t.shape, 1)
            gains = jnp.sum(jnp.where(pair_lane == pair, gain_t, 0.0), axis=1, keepdims=True)
            for half in range(2):
                head = 2 * pair + half
                own = pl.ds(pl.multiple_of(head * HEAD_DIM, HEAD_DIM), HEAD_DIM)
                rows = slice(half * HEAD_DIM, (half + 1) * HEAD_DIM)
                value = numer[own, :] + jnp.dot(state_t[rows], feat_q[head], preferred_element_type=F32)
                spread = jnp.sum(value * value, axis=0, keepdims=True) * (1.0 / HEAD_DIM)
                scaled = value * lax.rsqrt(spread + 1e-05) * gains[rows]
                numer[own, :] = scaled
            cols = pl.ds(pl.multiple_of(pair * PAIR, PAIR), PAIR)
            lin_out[:, cols] = numer[cols, :].T.astype(BF16)
            return carry

        lax.fori_loop(0, CHIPS, inter, 0, unroll=8)
        load_weight.wait()
        split = HEADS * HEAD_DIM
        acc[...] = jnp.dot(lin_out[...], weight[:split], preferred_element_type=F32)


    row = lax.broadcasted_iota(jnp.int32, (ROWS, ROWS), 0)
    col = lax.broadcasted_iota(jnp.int32, (ROWS, ROWS), 1)
    exp_scale = HEAD_DIM ** (-0.5) * 1.4426950408889634

    def output_copy(index):
        return remote(o_out.at[index], o_in.at[chip], o_ss.at[index], o_rs.at[chip], base + 8 * core + index)

    def arrive(index):
        @pl.when(has_earlier)
        def _():
            arrival(index).wait_recv()
            unpack(index)

        @pl.when(8 * core + index != place)
        def _():
            remote(qp_out.at[0], qp.at[index], qp_ss.at[0], qp_rs.at[index], me).wait_recv()

    def score(index, scores):
        packed_query = qp[index].astype(F32)
        query = jnp.concatenate([packed_query, pltpu.roll(packed_query, HEAD_DIM, 1)], axis=0).astype(BF16)
        raw = jnp.dot(query, kt[:, index * ROWS : index * ROWS + SPAN], preferred_element_type=F32)
        oldest = jnp.where(col > row, raw[:, :ROWS], -1e30)
        newest = jnp.where(col <= row, raw[:, WINDOW:], -1e30)
        scores[:, :ROWS] = oldest
        scores[:, ROWS:WINDOW] = raw[:, ROWS:WINDOW]
        scores[:, WINDOW:] = newest
        high = jnp.maximum(oldest, newest)
        for start in range(ROWS, WINDOW, ROWS):
            high = jnp.maximum(high, raw[:, start : start + ROWS])
        return jnp.max(high, axis=1, keepdims=True)

    def attend(index, scores, highest):
        weights = jnp.exp2((scores[...] - highest) * exp_scale).astype(BF16)
        sums = jnp.dot(weights, vo[index * ROWS : index * ROWS + SPAN, :], preferred_element_type=F32)
        result = sums / pltpu.roll(sums, HEAD_DIM, 1)
        packed = jnp.where(half_lane, pltpu.roll(result[:128], HEAD_DIM, 1), result[128:])
        o_out[index] = packed.astype(BF16)

    def send_output(index):
        @pl.when(8 * core + index != place)
        def _():
            output_copy(index).start()

        @pl.when(8 * core + index == place)
        def _():
            o_in[chip] = o_out[index]

    buffers = (scores_a, scores_b)
    arrive(7)
    highest = score(7, buffers[0])
    for turn in range(8):
        index = 7 - turn
        if turn == 8:
            inter_all()
        if index > 0:
            arrive(index - 1)
            next_highest = score(index - 1, buffers[(turn + 1) % 2])
        attend(index, buffers[turn % 2], highest)
        highest = next_highest
        send_output(index)
    inter_all()

    for head in range(WIN_HEADS):

        @pl.when(jnp.logical_or(head != chip, jnp.logical_not(stays)))
        def _():
            remote(o_out.at[0], o_in.at[head], o_ss.at[0], o_rs.at[head], me).wait_recv()

    tops, bottoms = [], []
    for pair in range(4):
        first = o_in[2 * pair].astype(F32)
        second = o_in[2 * pair + 1].astype(F32)
        tops.append(jnp.where(half_lane, first, pltpu.roll(second, HEAD_DIM, 1)).astype(BF16))
        bottoms.append(jnp.where(half_lane, pltpu.roll(first, HEAD_DIM, 1), second).astype(BF16))
    window_out = jnp.concatenate(
        [jnp.concatenate(tops, axis=1), jnp.concatenate(bottoms, axis=1)], axis=0
    )
    out_ref[...] = (acc[...] + jnp.dot(window_out, weight[HEADS * HEAD_DIM:], preferred_element_type=F32)).astype(BF16)

    for step in order:
        kv_copy(step).wait_send()
        qp_copy(step).wait_send()

    @pl.when(jnp.logical_not(stays))
    def _():
        kv_copy(0).wait_send()
        qp_copy(0).wait_send()

    @pl.when(passes_on)
    def _():
        for index in range(8):
            onward(index).wait_send()

    for index in range(8):

        @pl.when(8 * core + index != place)
        def _():
            output_copy(index).wait_send()


def per_device(lin_query, lin_key, lin_value, win_query, win_key, win_value, head_gain, out_weight):
    lines = lax.axis_size("seq") // LINE
    vmem = pl.BlockSpec(memory_space=pltpu.VMEM)
    hbm = pl.BlockSpec(memory_space=pl.ANY)
    tokens = (lin_query, lin_key, lin_value, win_query, win_key, win_value)
    dma = pltpu.SemaphoreType.DMA
    width = HEADS * HEAD_DIM
    scratch = [
        *[pltpu.VMEM(array.shape, BF16) for array in tokens],
        pltpu.VMEM(out_weight.shape, BF16),
        pltpu.VMEM((WIN_HEADS, ROWS, PAIR), BF16),
        pltpu.VMEM((WIN_HEADS, ROWS // 2, PAIR), BF16),
        pltpu.VMEM((SLOTS, ROWS, PAIR), BF16),
        pltpu.VMEM((8, ROWS // 2, PAIR), BF16),
        pltpu.VMEM((2 * HEAD_DIM, SLOTS * ROWS), BF16),
        pltpu.VMEM((SLOTS * ROWS, PAIR), BF16),
        pltpu.VMEM((ROWS, ROWS), F32),
        pltpu.VMEM((ROWS, ROWS), F32),
        pltpu.VMEM((width, ROWS), BF16),
        pltpu.VMEM((HEADS, FEATS, ROWS), BF16),
        pltpu.VMEM((width, ROWS), F32),
        pltpu.VMEM((ROWS, width), BF16),
        pltpu.VMEM((2, CHIPS, HALF, PAIR), BF16),
        pltpu.VMEM((CHIPS, HALF, PAIR), BF16),
        pltpu.VMEM((CHIPS, HALF, PAIR), BF16),
        pltpu.VMEM((CHIPS, HALF, PAIR), BF16),
        pltpu.VMEM((HALF, PAIR), BF16),
        pltpu.VMEM((lines - 1, HALF, PAIR), BF16),
        pltpu.VMEM((CHIPS, HALF, PAIR), BF16),
        pltpu.VMEM((CHIPS, HALF, PAIR), BF16),
        pltpu.VMEM((CHIPS, HALF, PAIR), BF16),
        pltpu.VMEM((2, CHIPS, HALF, PAIR), BF16),
        pltpu.VMEM((8, 128, PAIR), BF16),
        pltpu.VMEM((WIN_HEADS, 128, PAIR), BF16),
        pltpu.VMEM((ROWS, out_weight.shape[1]), F32),
        pltpu.VMEM((ROWS, SPAN), F32),
        pltpu.VMEM((ROWS, SPAN), F32),
        dma((7,)),
        dma((8,)), dma((SLOTS,)), dma((8,)), dma((8,)), dma((8,)), dma((8,)), dma((8,)),
        dma(()), dma(()),
        dma((8,)), dma((8,)),
        dma((lines - 1,)), dma((lines - 1,)),
        dma((8,)), dma((8,)),
        dma(()), dma(()),
    ]
    return pl.pallas_call(
        functools.partial(layer_kernel, lines),
        out_shape=pltpu.VMEM((ROWS, out_weight.shape[1]), BF16),
        in_specs=[hbm] * 6 + [vmem, hbm],
        out_specs=vmem,
        scratch_shapes=scratch,
        name="layer_pair",
        compiler_params=pltpu.CompilerParams(
            collective_id=0, has_side_effects=True, vmem_limit_bytes=56 * 2**20
        ),
    )(lin_query, lin_key, lin_value, win_query, win_key, win_value, head_gain.reshape(8, 128), out_weight)


def solution(mesh):
    rows = P(("doc", "seq"), None)
    return jax.shard_map(
        per_device,
        mesh=mesh,
        in_specs=(rows, rows, rows, rows, rows, rows, P(), P()),
        out_specs=rows,
        check_vma=False,
    )
```
